32 devices in a mesh: groups: 2 (over y), inst: 4 (over x, core), tp: 4 (over z).
Axes of the slice: x: 2, y: 2, z: 4, core: 2. Of those that a mesh axis runs over, the one named last changes fastest.
Arguments:
- prompt_blocks: bfloat16 [256, 2, 128, 1024], P(('groups', 'inst'), None, None, 'tp'), parts along dimension 0, may hold values from -9 to 9
- block_dest: int32 [256], P(('groups', 'inst')), parts along dimension 0, may hold values from 0 to 3, as said below
- block_slot: int32 [256], P(('groups', 'inst')), parts along dimension 0, may hold values from 0 to 63, as said below
- resident_cache: bfloat16 [16, 32, 2, 128, 1024], P(('groups', 'inst'), 'tp'), parts along dimension 0, may hold values from -9 to 9
- queries: bfloat16 [32, 8192], P(('groups', 'inst')), parts along dimension 0, may hold values from -32 to 32
- context_length: int32 [32], P(('groups', 'inst')), parts along dimension 0, may hold values from 1 to 4096, as said below
Outputs:
- attended: bfloat16 [32, 8192], P(('groups', 'inst'), 'tp'), parts along dimension 0
- installed: bfloat16 [16, 32, 2, 128, 1024], P(('groups', 'inst'), 'tp'), parts along dimension 0
The draws below stay inside these ranges and needn't reach their ends.
There are 2 independent parts, one for each index of `groups`. The reference program is written for one: setup_inputs(seed, part) draws one part's arguments, and reference() takes and returns one part's arrays. A program takes and returns all parts, laid end to end along the dimension named above; each array names one. Nothing has to cross between parts.
Inputs may be any that keep to these rules, and one draw needn't show every extreme that they name: `block_dest`: blocks k * 32 to (k + 1) * 32 - 1 are the prompt of instance k. At most 16 blocks of one instance's prompt name the same receiving instance, and in every prompt one receiving instance is named exactly 16 times. `block_slot`: blocks sent to one instance name distinct slots; slot q is page q % 32 of that instance's sequence q // 32. `context_length`: the 2 rows of a sequence are consecutive, their lengths rise by one from step to step, and in every instance one sequence's last row sees all 4096 positions.
All inputs are finite; a program needn't handle non-finite values.
Results may differ from the reference program's by a relative error of at most 0.001.
Values may be sent and summed in bfloat16 or wider, within the bound.
A program may use at most 128 MiB of HBM per device.

```python
import jax
import jax.numpy as jnp
from jax import lax

H = 64
KVH = 8
HD = 128
BT = 128
STEPS = 2
PAGES_SEQ = 32
BLK = 32
SEQ = 2
N_INST = 4


def block_plan(key):
    capacity = 2 * BLK // N_INST
    main_key, fill_key, order_key, slot_key = jax.random.split(key, 4)
    favored = jax.random.randint(main_key, (N_INST,), 0, N_INST)
    others = (favored[:, None] + 1 + jnp.arange((N_INST - 1) * capacity, dtype=jnp.int32)[None, :] // capacity) % N_INST
    shuffled = jax.vmap(jax.random.permutation)(jax.random.split(fill_key, N_INST), others)
    picked = jnp.concatenate([jnp.broadcast_to(favored[:, None], (N_INST, capacity)), shuffled[:, :BLK - capacity]], axis=1)
    destinations = jax.vmap(jax.random.permutation)(jax.random.split(order_key, N_INST), picked).reshape(-1).astype(jnp.int32)
    onehot = (destinations[:, None] == jnp.arange(N_INST, dtype=jnp.int32)[None, :]).astype(jnp.int32)
    arrival = jnp.sum((jnp.cumsum(onehot, axis=0) - onehot) * onehot, axis=1)

    def ordering(sub_key):
        return jax.random.permutation(sub_key, SEQ * PAGES_SEQ)
    orderings = jax.vmap(ordering)(jax.random.split(slot_key, N_INST))
    slot_ids = orderings[destinations, arrival].astype(jnp.int32)
    return (destinations, slot_ids)


def draw_block_dest(key, part):
    return block_plan(key)[0]


def draw_block_slot(key, part):
    return block_plan(key)[1]


def draw_prompt_blocks(key, part):
    key = jax.random.fold_in(key, 13)
    array_shape = (N_INST * BLK, 2, BT, KVH * HD)
    values = jnp.clip(jax.random.normal(key, array_shape, jnp.float32), -6.0, 6.0)
    return values.astype(jnp.bfloat16)


def draw_resident_cache(key, part):
    key = jax.random.fold_in(key, 11)
    array_shape = (N_INST * SEQ, PAGES_SEQ, 2, BT, KVH * HD)
    values = jnp.clip(jax.random.normal(key, array_shape, jnp.float32), -6.0, 6.0)
    return values.astype(jnp.bfloat16)


def draw_queries(key, part):
    key = jax.random.fold_in(key, 7)
    row_total = N_INST * SEQ * STEPS
    array_shape = (row_total, H * HD)
    values = 2.5 * jnp.clip(jax.random.normal(key, array_shape, jnp.float32), -4.0, 4.0)
    return values.astype(jnp.bfloat16)


def draw_context_length(key, part):
    key = jax.random.fold_in(key, 5)
    length_key, longest_key = jax.random.split(key)
    longest_len = PAGES_SEQ * BT
    opening = jax.random.randint(length_key, (N_INST, SEQ), 1, longest_len - STEPS + 2)
    longest = jax.random.randint(longest_key, (N_INST,), 0, SEQ)
    opening = jnp.where(jnp.arange(SEQ, dtype=jnp.int32)[None, :] == longest[:, None], longest_len - STEPS + 1, opening)
    row_lengths = opening[:, :, None] + jnp.arange(STEPS, dtype=jnp.int32)[None, None, :]
    return row_lengths.reshape(-1).astype(jnp.int32)


def setup_inputs(seed: int = 0, part: int = 0) -> dict:
    seeds = jax.random.split(jax.random.key(seed), 7)
    part_splits = jax.random.split(jax.random.fold_in(seeds[6], part), 7)
    prompt_blocks = draw_prompt_blocks(jax.random.fold_in(jax.random.fold_in(seeds[6], part), 71), part)
    block_dest = draw_block_dest(jax.random.fold_in(jax.random.fold_in(seeds[6], part), 71), part)
    block_slot = draw_block_slot(jax.random.fold_in(jax.random.fold_in(seeds[6], part), 71), part)
    resident_cache = draw_resident_cache(jax.random.fold_in(jax.random.fold_in(seeds[6], part), 71), part)
    queries = draw_queries(jax.random.fold_in(jax.random.fold_in(seeds[6], part), 71), part)
    context_length = draw_context_length(jax.random.fold_in(jax.random.fold_in(seeds[6], part), 71), part)
    return dict(prompt_blocks=prompt_blocks, block_dest=block_dest, block_slot=block_slot, resident_cache=resident_cache, queries=queries, context_length=context_length)


masked_score = -1.0e30


def reference(prompt_blocks, block_dest, block_slot, resident_cache, queries, context_length):
    seq_of = block_dest * SEQ + block_slot // PAGES_SEQ
    page_of = block_slot % PAGES_SEQ
    installed = resident_cache.at[seq_of, page_of].set(prompt_blocks)
    grouped = queries.reshape(N_INST * SEQ, STEPS, KVH, H // KVH, HD)
    length_rows = context_length.reshape(N_INST * SEQ, STEPS)
    positions = jnp.arange(PAGES_SEQ * BT, dtype=jnp.int32)

    def attend_one(operands):
        query_rows, page_rows, length_now = operands
        key_rows = page_rows[:, 0].reshape(PAGES_SEQ * BT, KVH, HD).astype(jnp.float32)
        value_rows = page_rows[:, 1].reshape(PAGES_SEQ * BT, KVH, HD).astype(jnp.float32)
        scores = jnp.einsum("evgd,kvd->evgk", query_rows.astype(jnp.float32), key_rows, precision=lax.Precision.HIGHEST) * (HD ** -0.5)
        usable = (positions[None, :] < length_now[:, None])[:, None, None, :]
        peak = jnp.max(jnp.where(usable, scores, masked_score), axis=-1, keepdims=True)
        weights = jnp.where(usable, jnp.exp(scores - peak), 0.0)
        denominator = jnp.sum(weights, axis=-1)
        numerator = jnp.einsum("evgk,kvd->evgd", weights, value_rows, precision=lax.Precision.HIGHEST)
        return (numerator / denominator[..., None]).astype(jnp.bfloat16)

    attended = lax.map(attend_one, (grouped, installed, length_rows))
    return attended.reshape(N_INST * SEQ * STEPS, H * HD), installed
```

```python
import functools

import jax
import jax.numpy as jnp
from jax import lax
from jax.experimental import pallas as pl
from jax.experimental.pallas import tpu as pltpu
from jax.sharding import PartitionSpec as P

H = 64
KVH = 8
HD = 128
STEPS = 2
GROUP = H // KVH
CORES = 2
PIECES = 8
MIB = 1024 * 1024

masked_score = -1e30
MESH_ID = pl.DeviceIdType.MESH


def migrate_kernel(
    insts, tps, share, index_ref, prompt_ref, page_ref, packed,
    x_send, x_recv, own_send, own_recv, hop_send, hop_recv,
    z_send, z_recv, back_send, back_recv, local_sem, keep_sem, *gathered,
):
    me = lax.axis_index("inst")
    tp = lax.axis_index("tp")
    core = lax.rem(me, CORES)
    chip = me // CORES
    chips = insts // CORES
    partner = me + 1 - 2 * core
    blocks, rows, width = prompt_ref.shape
    piece = rows // PIECES

    def mirror(step):
        return lax.rem(chip + step, chips) * CORES + core

    def tp_peer(step):
        return lax.rem(tp + step, tps)

    barrier = pltpu.get_barrier_semaphore()
    pl.semaphore_signal(barrier, inc=1, device_id={"inst": partner}, device_id_type=MESH_ID)
    for step in range(1, chips):
        pl.semaphore_signal(barrier, inc=1, device_id={"inst": mirror(step)}, device_id_type=MESH_ID)
    for step in range(1, tps):
        pl.semaphore_signal(barrier, inc=1, device_id={"tp": tp_peer(step)}, device_id_type=MESH_ID)
    pl.semaphore_wait(barrier, chips + tps - 1)

    def span(c):
        return pl.ds(c * piece, piece)

    def remote(src, dst, send, recv, where):
        return pltpu.make_async_remote_copy(
            src_ref=src, dst_ref=dst, send_sem=send, recv_sem=recv,
            device_id=where, device_id_type=MESH_ID,
        )

    def place(inst):
        return pl.ds(inst * blocks, blocks)

    def cross(c):
        src = prompt_ref.at[:, span(c), :]
        dst = gathered[c].at[place(me)]
        return [
            remote(src, dst, x_send.at[c, s - 1], x_recv.at[c, s - 1], {"inst": mirror(s)})
            for s in range(1, chips)
        ]

    def own(c):
        src = prompt_ref.at[:, span(c), :]
        dst = gathered[c].at[place(me)]
        return (
            remote(src, dst, own_send.at[c], own_recv.at[c], {"inst": partner}),
            pltpu.make_async_copy(src, dst, local_sem.at[c]),
        )

    def hop(c, s):
        origin = lax.rem(chip + chips - s, chips) * CORES + core
        part = gathered[c].at[place(origin)]
        return remote(part, part, hop_send.at[c, s - 1], hop_recv.at[c, s - 1], {"inst": partner})

    def spread(c):
        copies = []
        dst = page_ref.at[
            pl.ds(core * share, share), span(c), pl.ds(pl.multiple_of(tp * width, 128), width)
        ]
        for s in range(1, tps):
            peer = tp_peer(s)
            src = packed.at[pl.ds(peer * share, share), span(c), :]
            copies.append(
                remote(src, dst, z_send.at[c, s - 1], z_recv.at[c, s - 1], {"tp": peer})
            )
        kept = packed.at[pl.ds(tp * share, share), span(c), :]
        return copies, pltpu.make_async_copy(kept, dst, keep_sem.at[c])

    def back(c):
        part = page_ref.at[pl.ds(core * share, share), span(c), :]
        return remote(part, part, back_send.at[c], back_recv.at[c], {"inst": partner})

    def begin(c):
        for copy in cross(c):
            copy.start()
        for copy in own(c):
            copy.start()

    def finish_spread(c):
        copies, kept = spread(c)
        for copy in copies:
            copy.wait_recv()
        kept.wait()
        back(c).start()

    begin(0)
    begin(1)
    for c in range(PIECES):
        if c + 2 < PIECES:
            begin(c + 2)
        crossing = cross(c)
        for s in range(1, chips):
            crossing[s - 1].wait_recv()
            hop(c, s).start()
        to_partner, kept = own(c)
        kept.wait()
        to_partner.wait_recv()
        for s in range(1, chips):
            hop(c, s).wait_recv()

        def pack(entry, carry):
            packed[entry, span(c), :] = gathered[c][index_ref[entry]]
            return carry

        lax.fori_loop(0, tps * share, pack, 0)
        copies, kept = spread(c)
        for copy in copies:
            copy.start()
        kept.start()
        if c >= 1:
            finish_spread(c - 1)
    finish_spread(PIECES - 1)
    for c in range(PIECES):
        for copy in cross(c):
            copy.wait_send()
        own(c)[0].wait_send()
        for s in range(1, chips):
            hop(c, s).wait_send()
        for copy in spread(c)[0]:
            copy.wait_send()
        back(c).wait()


def migrate(index, prompt, insts, tps, share, collective_id):
    blocks, rows, width = prompt.shape
    chips = insts // CORES
    dma = pltpu.SemaphoreType.DMA
    return pl.pallas_call(
        functools.partial(migrate_kernel, insts, tps, share),
        out_shape=jax.ShapeDtypeStruct((CORES * share, rows, width * tps), prompt.dtype),
        in_specs=[
            pl.BlockSpec(memory_space=pltpu.SMEM),
            pl.BlockSpec(memory_space=pl.ANY),
        ],
        out_specs=pl.BlockSpec(memory_space=pl.ANY),
        scratch_shapes=[
            pltpu.VMEM((tps * share, rows, width), prompt.dtype),
            dma((PIECES, chips - 1)), dma((PIECES, chips - 1)),
            dma((PIECES,)), dma((PIECES,)),
            dma((PIECES, chips - 1)), dma((PIECES, chips - 1)),
            dma((PIECES, tps - 1)), dma((PIECES, tps - 1)),
            dma((PIECES,)), dma((PIECES,)),
            dma((PIECES,)), dma((PIECES,)),
        ]
        + [pltpu.VMEM((insts * blocks, rows // PIECES, width), prompt.dtype)] * PIECES,
        compiler_params=pltpu.CompilerParams(
            collective_id=collective_id, has_side_effects=True, vmem_limit_bytes=48 * MIB
        ),
        name="migrate",
    )(index, prompt)


def attend_kernel(
    page_local, flag_ref, place_ref, length_ref, base_ref,
    page_ref, resident_ref, query_ref, out_ref, state_ref,
):
    step = pl.program_id(0)
    seq = step // page_local
    page = lax.rem(step, page_local)
    fresh = flag_ref[step] > 0

    @pl.when(fresh)
    def _():
        out_ref[...] = page_ref[...]

    @pl.when(jnp.logical_not(fresh))
    def _():
        out_ref[...] = resident_ref[...]

    @pl.when(page == 0)
    def _():
        state_ref[0, 0] = jnp.full(state_ref.shape[2:], masked_score, jnp.float32)
        state_ref[0, 1] = jnp.zeros(state_ref.shape[2:], jnp.float32)
        state_ref[0, 2] = jnp.zeros(state_ref.shape[2:], jnp.float32)

    tokens = out_ref.shape[1] // 2
    keys = out_ref[0, :tokens, :]
    scores = lax.dot_general(
        query_ref[0], keys, (((1,), (1,)), ((), ())), preferred_element_type=jnp.float32
    ) * HD ** (-0.5)
    row = lax.broadcasted_iota(jnp.int32, scores.shape, 0)
    position = base_ref[0] + page * tokens + lax.broadcasted_iota(jnp.int32, scores.shape, 1)
    decode_step = lax.rem(row // GROUP, STEPS)
    limit = jnp.full(scores.shape, length_ref[seq * STEPS], jnp.int32)
    for e in range(1, STEPS):
        limit = jnp.where(decode_step == e, length_ref[seq * STEPS + e], limit)
    usable = position < limit
    old_peak = state_ref[0, 0]
    best = jnp.max(jnp.where(usable, scores, masked_score), axis=1, keepdims=True)
    peak = jnp.maximum(old_peak, best)
    factor = jnp.exp(old_peak - peak)
    weights = jnp.where(usable, jnp.exp(scores - peak[:, :1]), 0.0)
    state_ref[0, 0] = peak
    state_ref[0, 1] = state_ref[0, 1] * factor + jnp.sum(weights, axis=1, keepdims=True)
    high = weights.astype(jnp.bfloat16)
    low = (weights - high.astype(jnp.float32)).astype(jnp.bfloat16)
    rows = STEPS * GROUP
    for v in range(KVH):
        values = out_ref[0, tokens:, v * HD : (v + 1) * HD]
        part = slice(v * rows, (v + 1) * rows)
        both = jnp.concatenate([high[part], low[part]], axis=0)
        product = jnp.dot(both, values, preferred_element_type=jnp.float32)
        state_ref[0, 2, part, :] = (
            state_ref[0, 2, part, :] * factor[part] + product[:rows] + product[rows:]
        )


def attend(flags, places, lengths, base, pages, resident, queries, seqs):
    total, rows, width = resident.shape
    page_local = total // seqs
    heads = KVH * STEPS * GROUP
    grid_spec = pltpu.PrefetchScalarGridSpec(
        num_scalar_prefetch=4,
        grid=(total,),
        in_specs=[
            pl.BlockSpec((1, rows, width), lambda s, f, p, l, b: (p[s], 0, 0)),
            pl.BlockSpec((1, rows, width), lambda s, f, p, l, b: (s, 0, 0)),
            pl.BlockSpec((1, heads, KVH * HD), lambda s, f, p, l, b: (s // page_local, 0, 0)),
        ],
        out_specs=[
            pl.BlockSpec((1, rows, width), lambda s, f, p, l, b: (s, 0, 0)),
            pl.BlockSpec((1, 3, heads, HD), lambda s, f, p, l, b: (s // page_local, 0, 0, 0)),
        ],
    )
    return pl.pallas_call(
        functools.partial(attend_kernel, page_local),
        grid_spec=grid_spec,
        out_shape=[
            jax.ShapeDtypeStruct(resident.shape, resident.dtype),
            jax.ShapeDtypeStruct((seqs, 3, heads, HD), jnp.float32),
        ],
        compiler_params=pltpu.CompilerParams(vmem_limit_bytes=32 * MIB),
        name="attend",
    )(flags, places, lengths, base, pages, resident, queries)


def combine_kernel(tps, state_ref, out_ref, arrived, send_sem, recv_sem):
    tp = lax.axis_index("tp")
    rows = out_ref.shape[1]
    barrier = pltpu.get_barrier_semaphore()
    for s in range(1, tps):
        pl.semaphore_signal(
            barrier, inc=1, device_id={"tp": lax.rem(tp + s, tps)}, device_id_type=MESH_ID
        )
    pl.semaphore_wait(barrier, tps - 1)
    copies = []
    for s in range(1, tps):
        peer = lax.rem(tp + s, tps)
        copies.append(
            pltpu.make_async_remote_copy(
                src_ref=state_ref.at[:, :, pl.ds(pl.multiple_of(peer * rows, 8), rows), :],
                dst_ref=arrived.at[s - 1],
                send_sem=send_sem.at[s - 1],
                recv_sem=recv_sem.at[s - 1],
                device_id={"tp": peer},
                device_id_type=MESH_ID,
            )
        )
    for copy in copies:
        copy.start()
    mine = state_ref[:, :, pl.ds(pl.multiple_of(tp * rows, 8), rows), :]
    peak, denominator, numerator = mine[:, 0], mine[:, 1], mine[:, 2]
    for s in range(1, tps):
        copies[s - 1].wait()
        other = arrived[s - 1]
        joint = jnp.maximum(peak, other[:, 0])
        here = jnp.exp(peak - joint)
        there = jnp.exp(other[:, 0] - joint)
        denominator = denominator * here + other[:, 1] * there
        numerator = numerator * here + other[:, 2] * there
        peak = joint
    out_ref[...] = (numerator / denominator).astype(out_ref.dtype)


def combine(state, tps):
    seqs, kinds, heads, size = state.shape
    rows = heads // tps
    return pl.pallas_call(
        functools.partial(combine_kernel, tps),
        out_shape=jax.ShapeDtypeStruct((seqs, rows, size), jnp.bfloat16),
        in_specs=[pl.BlockSpec(memory_space=pltpu.VMEM)],
        out_specs=pl.BlockSpec(memory_space=pltpu.VMEM),
        scratch_shapes=[
            pltpu.VMEM((tps - 1, seqs, kinds, rows, size), jnp.float32),
            pltpu.SemaphoreType.DMA((tps - 1,)),
            pltpu.SemaphoreType.DMA((tps - 1,)),
        ],
        compiler_params=pltpu.CompilerParams(collective_id=1, has_side_effects=True),
        name="combine",
    )(state)


def on_device(prompt_blocks, block_dest, block_slot, resident_cache, queries, context_length):
    insts = lax.axis_size("inst")
    tps = lax.axis_size("tp")
    me = lax.axis_index("inst")
    tp = lax.axis_index("tp")
    blocks, kinds, tokens, width = prompt_blocks.shape
    seqs, page_local = resident_cache.shape[:2]
    pages_seq = page_local * tps
    share = seqs * page_local
    every = lax.all_gather(jnp.stack([block_dest, block_slot]), "inst", axis=1, tiled=True)
    dest, slot = every[0], every[1]
    total = insts * blocks
    holder = (slot % pages_seq) // page_local
    pool = (dest // CORES) * tps + holder
    order = jnp.arange(total, dtype=jnp.int32)
    rank = jnp.sum(
        jnp.logical_and(pool[:, None] == pool[None, :], order[None, :] < order[:, None]),
        axis=1,
        dtype=jnp.int32,
    )
    entry = jnp.arange(tps * share, dtype=jnp.int32)
    entry_pool = (me // CORES) * tps + entry // share
    entry_rank = (entry % share) * CORES + me % CORES
    hits = jnp.logical_and(pool[None, :] == entry_pool[:, None], rank[None, :] == entry_rank[:, None])
    index = jnp.sum(jnp.where(hits, order[None, :], 0), axis=1, dtype=jnp.int32)
    local = jnp.arange(share, dtype=jnp.int32)
    wanted = (local // page_local) * pages_seq + tp * page_local + local % page_local
    found = jnp.logical_and(dest[None, :] == me, slot[None, :] == wanted[:, None])
    spot = (rank % CORES) * share + rank // CORES
    places = jnp.sum(jnp.where(found, spot[None, :], 0), axis=1, dtype=jnp.int32)
    flags = jnp.any(found, axis=1).astype(jnp.int32)

    prompt = prompt_blocks.reshape(blocks, kinds * tokens, width)
    pages = migrate(index, prompt, insts, tps, share, 0)

    by_head = queries.reshape(seqs, STEPS, KVH, GROUP, HD).transpose(0, 2, 1, 3, 4)
    by_head = by_head.reshape(seqs, KVH, STEPS * GROUP, 1, HD)
    diagonal = jnp.eye(KVH, dtype=jnp.bool_)[None, :, None, :, None]
    wide = jnp.where(diagonal, by_head, jnp.zeros((), queries.dtype))
    wide = wide.reshape(seqs, KVH * STEPS * GROUP, KVH * HD)
    base = (tp * pages_seq // tps * tokens).astype(jnp.int32).reshape(1)
    resident = resident_cache.reshape(share, kinds * tokens, width * tps)
    installed, state = attend(flags, places, context_length, base, pages, resident, wide, seqs)
    merged = combine(state, tps)
    attended = merged.reshape(seqs, KVH // tps, STEPS, GROUP, HD).transpose(0, 2, 1, 3, 4)
    attended = attended.reshape(seqs * STEPS, H * HD // tps)
    return attended, installed.reshape(resident_cache.shape)


def solution(mesh):
    in_specs = (
        P(("groups", "inst"), None, None, "tp"),
        P(("groups", "inst")),
        P(("groups", "inst")),
        P(("groups", "inst"), "tp", None, None, None),
        P(("groups", "inst"), None),
        P(("groups", "inst")),
    )
    out_specs = (P(("groups", "inst"), "tp"), P(("groups", "inst"), "tp", None, None, None))
    return jax.shard_map(
        on_device, mesh=mesh, in_specs=in_specs, out_specs=out_specs, check_vma=False
    )
```

```python
import functools

import jax
import jax.numpy as jnp
from jax import lax
from jax.experimental import pallas as pl
from jax.experimental.pallas import tpu as pltpu
from jax.sharding import PartitionSpec as P

H = 64
KVH = 8
HD = 128
STEPS = 2
GROUP = H // KVH
CORES = 2
PARTS = (1, 1, 2, 2, 2, 2, 2, 2, 1, 1)
PIECES = len(PARTS)
LEVELS = (11, 12, 13, 16)
PAGES_STEP = 4
LANES = 128
MIB = 1024 * 1024

masked_score = -1e30
MESH_ID = pl.DeviceIdType.MESH


def migrate_kernel(
    insts, tps, share, sent, index_ref, prompt_ref, page_ref, packed,
    x_send, x_recv, own_send, own_recv, hop_send, hop_recv,
    z_send, z_recv, back_send, back_recv, local_sem, keep_sem, *gathered,
):
    me = lax.axis_index("inst")
    tp = lax.axis_index("tp")
    core = lax.rem(me, CORES)
    chip = me // CORES
    chips = insts // CORES
    partner = me + 1 - 2 * core
    blocks, rows, width = prompt_ref.shape
    unit = rows // sum(PARTS)

    def mirror(step):
        return lax.rem(chip + step, chips) * CORES + core

    def tp_peer(step):
        return lax.rem(tp + step, tps)

    barrier = pltpu.get_barrier_semaphore()
    pl.semaphore_signal(barrier, inc=1, device_id={"inst": partner}, device_id_type=MESH_ID)
    for step in range(1, chips):
        pl.semaphore_signal(barrier, inc=1, device_id={"inst": mirror(step)}, device_id_type=MESH_ID)
    for step in range(1, tps):
        pl.semaphore_signal(barrier, inc=1, device_id={"tp": tp_peer(step)}, device_id_type=MESH_ID)
    pl.semaphore_wait(barrier, chips + tps - 1)

    def span(c):
        return pl.ds(sum(PARTS[:c]) * unit, PARTS[c] * unit)

    def remote(src, dst, send, recv, where):
        return pltpu.make_async_remote_copy(
            src_ref=src, dst_ref=dst, send_sem=send, recv_sem=recv,
            device_id=where, device_id_type=MESH_ID,
        )

    def place(inst):
        return pl.ds(inst * blocks, blocks)

    def cross(c):
        src = prompt_ref.at[:, span(c), :]
        dst = gathered[c].at[place(me)]
        return [
            remote(src, dst, x_send.at[c, s - 1], x_recv.at[c, s - 1], {"inst": mirror(s)})
            for s in range(1, chips)
        ]

    def own(c):
        src = prompt_ref.at[:, span(c), :]
        dst = gathered[c].at[place(me)]
        return (
            remote(src, dst, own_send.at[c], own_recv.at[c], {"inst": partner}),
            pltpu.make_async_copy(src, dst, local_sem.at[c]),
        )

    def hop(c, s):
        origin = lax.rem(chip + chips - s, chips) * CORES + core
        part = gathered[c].at[place(origin)]
        return remote(part, part, hop_send.at[c, s - 1], hop_recv.at[c, s - 1], {"inst": partner})

    def spread(c):
        copies = []
        dst = page_ref.at[
            pl.ds(core * share, sent), span(c), pl.ds(pl.multiple_of(tp * width, 128), width)
        ]
        for s in range(1, tps):
            peer = tp_peer(s)
            src = packed.at[pl.ds(peer * sent, sent), span(c), :]
            copies.append(
                remote(src, dst, z_send.at[c, s - 1], z_recv.at[c, s - 1], {"tp": peer})
            )
        kept = packed.at[pl.ds(tp * sent, sent), span(c), :]
        return copies, pltpu.make_async_copy(kept, dst, keep_sem.at[c])

    def back(c):
        part = page_ref.at[pl.ds(core * share, sent), span(c), :]
        return remote(part, part, back_send.at[c], back_recv.at[c], {"inst": partner})

    def begin(c):
        for copy in cross(c):
            copy.start()
        for copy in own(c):
            copy.start()

    def finish_spread(c):
        copies, kept = spread(c)
        for copy in copies:
            copy.wait_recv()
        kept.wait()
        back(c).start()

    begin(0)
    begin(1)
    for c in range(PIECES):
        if c + 2 < PIECES:
            begin(c + 2)
        crossing = cross(c)
        for s in range(1, chips):
            crossing[s - 1].wait_recv()
            hop(c, s).start()
        to_partner, kept = own(c)
        kept.wait()
        to_partner.wait_recv()
        for s in range(1, chips):
            hop(c, s).wait_recv()

        def pack(entry, carry):
            chosen = index_ref[entry // sent * share + lax.rem(entry, sent)]
            packed[entry, span(c), :] = gathered[c][chosen]
            return carry

        lax.fori_loop(0, tps * sent, pack, 0)
        copies, kept = spread(c)
        for copy in copies:
            copy.start()
        kept.start()
        if c >= 1:
            finish_spread(c - 1)
    finish_spread(PIECES - 1)
    for c in range(PIECES):
        for copy in cross(c):
            copy.wait_send()
        own(c)[0].wait_send()
        for s in range(1, chips):
            hop(c, s).wait_send()
        for copy in spread(c)[0]:
            copy.wait_send()
        back(c).wait()


def migrate(insts, tps, share, sent, collective_id, index, prompt):
    blocks, rows, width = prompt.shape
    chips = insts // CORES
    dma = pltpu.SemaphoreType.DMA
    return pl.pallas_call(
        functools.partial(migrate_kernel, insts, tps, share, sent),
        out_shape=jax.ShapeDtypeStruct((CORES * share, rows, width * tps), prompt.dtype),
        in_specs=[
            pl.BlockSpec(memory_space=pltpu.SMEM),
            pl.BlockSpec(memory_space=pl.ANY),
        ],
        out_specs=pl.BlockSpec(memory_space=pl.ANY),
        scratch_shapes=[
            pltpu.VMEM((tps * sent, rows, width), prompt.dtype),
            dma((PIECES, chips - 1)), dma((PIECES, chips - 1)),
            dma((PIECES,)), dma((PIECES,)),
            dma((PIECES, chips - 1)), dma((PIECES, chips - 1)),
            dma((PIECES, tps - 1)), dma((PIECES, tps - 1)),
            dma((PIECES,)), dma((PIECES,)),
            dma((PIECES,)), dma((PIECES,)),
        ]
        + [
            pltpu.VMEM((insts * blocks, rows // sum(PARTS) * part, width), prompt.dtype)
            for part in PARTS
        ],
        compiler_params=pltpu.CompilerParams(
            collective_id=collective_id, has_side_effects=True, vmem_limit_bytes=48 * MIB
        ),
        name=f"migrate_{sent}",
    )(index, prompt)


def attend_kernel(page_local, flag_ref, place_ref, kept_ref, length_ref, base_ref, *refs):
    pages, residents = refs[:PAGES_STEP], refs[PAGES_STEP : 2 * PAGES_STEP]
    query_ref, out_ref, numerator_ref, stat_ref, peak_ref, denominator_ref = refs[2 * PAGES_STEP :]
    step = pl.program_id(0)
    seq = step * PAGES_STEP // page_local
    first = lax.rem(step * PAGES_STEP, page_local)

    for i in range(PAGES_STEP):
        fresh = flag_ref[step * PAGES_STEP + i] > 0

        @pl.when(fresh)
        def _():
            out_ref[i] = pages[i][0]

        @pl.when(jnp.logical_not(fresh))
        def _():
            out_ref[i] = residents[i][0]

    @pl.when(first == 0)
    def _():
        peak_ref[...] = jnp.full(peak_ref.shape, masked_score, jnp.float32)
        denominator_ref[...] = jnp.zeros(denominator_ref.shape, jnp.float32)
        numerator_ref[...] = jnp.zeros(numerator_ref.shape, jnp.float32)

    tokens = out_ref.shape[1] // 2
    scores = jnp.concatenate(
        [
            lax.dot_general(
                query_ref[0],
                out_ref[i, :tokens, :],
                (((1,), (1,)), ((), ())),
                preferred_element_type=jnp.float32,
            )
            for i in range(PAGES_STEP)
        ],
        axis=1,
    ) * HD ** (-0.5)
    row = lax.broadcasted_iota(jnp.int32, scores.shape, 0)
    start = base_ref[0] + first * tokens
    position = start + lax.broadcasted_iota(jnp.int32, scores.shape, 1)
    decode_step = lax.rem(row // GROUP, STEPS)
    limit = jnp.full(scores.shape, length_ref[seq * STEPS], jnp.int32)
    for e in range(1, STEPS):
        limit = jnp.where(decode_step == e, length_ref[seq * STEPS + e], limit)
    usable = position < limit
    old_peak = peak_ref[...]
    best = jnp.max(jnp.where(usable, scores, masked_score), axis=1, keepdims=True)
    peak = jnp.maximum(old_peak, best)
    factor = jnp.exp(old_peak - peak)
    weights = jnp.where(usable, jnp.exp(scores - peak[:, :1]), 0.0)
    denominator = denominator_ref[...] * factor + jnp.sum(weights, axis=1, keepdims=True)
    peak_ref[...] = peak
    denominator_ref[...] = denominator
    high = weights.astype(jnp.bfloat16)
    low = (weights - high.astype(jnp.float32)).astype(jnp.bfloat16)
    rows = STEPS * GROUP
    for v in range(KVH):
        part = slice(v * rows, (v + 1) * rows)
        both = jnp.concatenate([high[part], low[part]], axis=0)
        product = sum(
            jnp.dot(
                both[:, i * tokens : (i + 1) * tokens],
                out_ref[i, tokens:, v * HD : (v + 1) * HD],
                preferred_element_type=jnp.float32,
            )
            for i in range(PAGES_STEP)
        )
        numerator_ref[0, part, :] = (
            numerator_ref[0, part, :] * factor[part] + product[:rows] + product[rows:]
        )

    @pl.when(first == page_local - PAGES_STEP)
    def _():
        lane = lax.broadcasted_iota(jnp.int32, stat_ref.shape, 1)
        spot = lane // (LANES // 4)
        stats = jnp.where(spot == 2 * seq, peak, stat_ref[...])
        stat_ref[...] = jnp.where(spot == 2 * seq + 1, denominator, stats)


def attend(flags, places, kept, lengths, base, pages, resident, queries, seqs):
    total, rows, width = resident.shape
    page_local = total // seqs
    heads = KVH * STEPS * GROUP
    steps_seq = page_local // PAGES_STEP

    def page_spec(which, i):
        return pl.BlockSpec(
            (1, rows, width), lambda s, *scalars: (scalars[which][s * PAGES_STEP + i], 0, 0)
        )

    grid_spec = pltpu.PrefetchScalarGridSpec(
        num_scalar_prefetch=5,
        grid=(total // PAGES_STEP,),
        in_specs=[page_spec(1, i) for i in range(PAGES_STEP)]
        + [page_spec(2, i) for i in range(PAGES_STEP)]
        + [pl.BlockSpec((1, heads, KVH * HD), lambda s, *scalars: (s // steps_seq, 0, 0))],
        out_specs=[
            pl.BlockSpec((PAGES_STEP, rows, width), lambda s, *scalars: (s, 0, 0)),
            pl.BlockSpec((1, heads, HD), lambda s, *scalars: (s // steps_seq, 0, 0)),
            pl.BlockSpec((heads, LANES), lambda s, *scalars: (0, 0)),
        ],
        scratch_shapes=[pltpu.VMEM((heads, LANES), jnp.float32)] * 2,
    )
    return pl.pallas_call(
        functools.partial(attend_kernel, page_local),
        grid_spec=grid_spec,
        out_shape=[
            jax.ShapeDtypeStruct(resident.shape, resident.dtype),
            jax.ShapeDtypeStruct((seqs, heads, HD), jnp.float32),
            jax.ShapeDtypeStruct((heads, LANES), jnp.float32),
        ],
        compiler_params=pltpu.CompilerParams(vmem_limit_bytes=40 * MIB),
        name="attend",
    )(
        flags, places, kept, lengths, base,
        *[pages] * PAGES_STEP, *[resident] * PAGES_STEP, queries,
    )


def combine_kernel(tps, numerator_ref, stat_ref, out_ref, arrived, arrived_stat, send_sem, recv_sem):
    tp = lax.axis_index("tp")
    seqs, rows = out_ref.shape[:2]
    barrier = pltpu.get_barrier_semaphore()
    for s in range(1, tps):
        pl.semaphore_signal(
            barrier, inc=1, device_id={"tp": lax.rem(tp + s, tps)}, device_id_type=MESH_ID
        )
    pl.semaphore_wait(barrier, tps - 1)
    copies = []
    for s in range(1, tps):
        peer = lax.rem(tp + s, tps)
        part = pl.ds(pl.multiple_of(peer * rows, 8), rows)
        for kind, (src, dst) in enumerate(
            ((numerator_ref.at[:, part, :], arrived), (stat_ref.at[part, :], arrived_stat))
        ):
            copies.append(
                pltpu.make_async_remote_copy(
                    src_ref=src,
                    dst_ref=dst.at[s - 1],
                    send_sem=send_sem.at[kind, s - 1],
                    recv_sem=recv_sem.at[kind, s - 1],
                    device_id={"tp": peer},
                    device_id_type=MESH_ID,
                )
            )
    for copy in copies:
        copy.start()
    mine = pl.ds(pl.multiple_of(tp * rows, 8), rows)
    step = LANES // 4
    for copy in copies:
        copy.wait()
    for seq in range(seqs):
        stats = [stat_ref[mine, :]] + [arrived_stat[s] for s in range(tps - 1)]
        tops = [numerator_ref[seq, mine, :]] + [arrived[s, seq] for s in range(tps - 1)]
        peaks = [part[:, 2 * seq * step : 2 * seq * step + 1] for part in stats]
        lows = [part[:, (2 * seq + 1) * step : (2 * seq + 1) * step + 1] for part in stats]
        peak = functools.reduce(jnp.maximum, peaks)
        factors = [jnp.exp(part - peak) for part in peaks]
        numerator = sum(top * factor for top, factor in zip(tops, factors))
        denominator = sum(low * factor for low, factor in zip(lows, factors))
        out_ref[seq] = (numerator / denominator).astype(out_ref.dtype)


def combine(numerator, stats, tps, collective_id):
    seqs, heads, size = numerator.shape
    rows = heads // tps
    return pl.pallas_call(
        functools.partial(combine_kernel, tps),
        out_shape=jax.ShapeDtypeStruct((seqs, rows, size), jnp.bfloat16),
        in_specs=[pl.BlockSpec(memory_space=pltpu.VMEM)] * 2,
        out_specs=pl.BlockSpec(memory_space=pltpu.VMEM),
        scratch_shapes=[
            pltpu.VMEM((tps - 1, seqs, rows, size), jnp.float32),
            pltpu.VMEM((tps - 1, rows, LANES), jnp.float32),
            pltpu.SemaphoreType.DMA((2, tps - 1)),
            pltpu.SemaphoreType.DMA((2, tps - 1)),
        ],
        compiler_params=pltpu.CompilerParams(collective_id=collective_id, has_side_effects=True),
        name="combine",
    )(numerator, stats)


def on_device(prompt_blocks, block_dest, block_slot, resident_cache, queries, context_length):
    insts = lax.axis_size("inst")
    tps = lax.axis_size("tp")
    me = lax.axis_index("inst")
    tp = lax.axis_index("tp")
    blocks, kinds, tokens, width = prompt_blocks.shape
    seqs, page_local = resident_cache.shape[:2]
    pages_seq = page_local * tps
    share = seqs * page_local
    pairs = lax.all_gather(jnp.stack([block_dest, block_slot]), ("groups", "inst"))
    pairs = pairs.reshape((-1, insts) + pairs.shape[1:]).transpose(0, 2, 1, 3)
    pairs = pairs.reshape(pairs.shape[0], 2, insts * blocks)
    load = pairs[:, 0] // CORES * tps + pairs[:, 1] % pages_seq // page_local
    pools = jnp.arange(insts // CORES * tps, dtype=jnp.int32)
    counts = jnp.sum(load[:, :, None] == pools, axis=1, dtype=jnp.int32)
    needed = (jnp.max(counts) + CORES - 1) // CORES
    every = lax.dynamic_index_in_dim(pairs, lax.axis_index("groups"), 0, keepdims=False)
    dest, slot = every[0], every[1]
    total = insts * blocks
    holder = (slot % pages_seq) // page_local
    pool = (dest // CORES) * tps + holder
    order = jnp.arange(total, dtype=jnp.int32)
    rank = jnp.sum(
        jnp.logical_and(pool[:, None] == pool[None, :], order[None, :] < order[:, None]),
        axis=1,
        dtype=jnp.int32,
    )
    entry = jnp.arange(tps * share, dtype=jnp.int32)
    entry_pool = (me // CORES) * tps + entry // share
    entry_rank = (entry % share) * CORES + me % CORES
    hits = jnp.logical_and(pool[None, :] == entry_pool[:, None], rank[None, :] == entry_rank[:, None])
    index = jnp.sum(jnp.where(hits, order[None, :], 0), axis=1, dtype=jnp.int32)
    local = jnp.arange(share, dtype=jnp.int32)
    wanted = (local // page_local) * pages_seq + tp * page_local + local % page_local
    found = jnp.logical_and(dest[None, :] == me, slot[None, :] == wanted[:, None])
    spot = (rank % CORES) * share + rank // CORES
    places = jnp.sum(jnp.where(found, spot[None, :], 0), axis=1, dtype=jnp.int32)
    flags = jnp.any(found, axis=1).astype(jnp.int32)

    prompt = prompt_blocks.reshape(blocks, kinds * tokens, width)
    levels = sorted({-(-share * level // LEVELS[-1]) for level in LEVELS})
    variant = sum((needed > level).astype(jnp.int32) for level in levels[:-1])
    pages = lax.switch(
        variant,
        [
            functools.partial(migrate, insts, tps, share, sent, i)
            for i, sent in enumerate(levels)
        ],
        index,
        prompt,
    )
    place_rows, kept_rows = [], []
    place_now = kept_now = jnp.zeros((PAGES_STEP,), jnp.int32)
    for row in range(share // PAGES_STEP):
        part = slice(row * PAGES_STEP, (row + 1) * PAGES_STEP)
        fresh = flags[part] > 0
        place_now = jnp.where(fresh, places[part], place_now)
        kept_now = jnp.where(fresh, kept_now, local[part])
        place_rows.append(place_now)
        kept_rows.append(kept_now)
    places, kept = jnp.concatenate(place_rows), jnp.concatenate(kept_rows)

    by_head = queries.reshape(seqs, STEPS, KVH, GROUP, HD).transpose(0, 2, 1, 3, 4)
    by_head = by_head.reshape(seqs, KVH, STEPS * GROUP, 1, HD)
    diagonal = jnp.eye(KVH, dtype=jnp.bool_)[None, :, None, :, None]
    wide = jnp.where(diagonal, by_head, jnp.zeros((), queries.dtype))
    wide = wide.reshape(seqs, KVH * STEPS * GROUP, KVH * HD)
    base = (tp * pages_seq // tps * tokens).astype(jnp.int32).reshape(1)
    resident = resident_cache.reshape(share, kinds * tokens, width * tps)
    installed, numerator, stats = attend(
        flags, places, kept, context_length, base, pages, resident, wide, seqs
    )
    merged = combine(numerator, stats, tps, len(levels))
    attended = merged.reshape(seqs, KVH // tps, STEPS, GROUP, HD).transpose(0, 2, 1, 3, 4)
    attended = attended.reshape(seqs * STEPS, H * HD // tps)
    return attended, installed.reshape(resident_cache.shape)


def solution(mesh):
    in_specs = (
        P(("groups", "inst"), None, None, "tp"),
        P(("groups", "inst")),
        P(("groups", "inst")),
        P(("groups", "inst"), "tp", None, None, None),
        P(("groups", "inst"), None),
        P(("groups", "inst")),
    )
    out_specs = (P(("groups", "inst"), "tp"), P(("groups", "inst"), "tp", None, None, None))
    return jax.shard_map(
        on_device, mesh=mesh, in_specs=in_specs, out_specs=out_specs, check_vma=False
    )
```

```python
import functools

import jax
import jax.numpy as jnp
from jax import lax
from jax.experimental import pallas as pl
from jax.experimental.pallas import tpu as pltpu
from jax.sharding import PartitionSpec as P

H = 64
KVH = 8
HD = 128
STEPS = 2
GROUP = H // KVH
CORES = 2
PARTS = (1,) * 16
PIECES = len(PARTS)
LEVELS = (11, 12, 13, 16)
PAGES_STEP = 4
LANES = 128
MIB = 1024 * 1024

masked_score = -1e30
MESH_ID = pl.DeviceIdType.MESH


def opening_kernel(
    groups, insts, plan_ref, prompt_ref, every_ref, first_ref,
    plan_send, plan_recv, x_send, x_recv, own_send, own_recv, hop_send, hop_recv, local_sem,
):
    group = lax.axis_index("groups")
    me = lax.axis_index("inst")
    core = lax.rem(me, CORES)
    chip = me // CORES
    chips = insts // CORES
    partner = me + 1 - 2 * core
    blocks = prompt_ref.shape[0]
    rows = first_ref.shape[1]
    peers = []
    for g in range(groups):
        for i in range(insts):
            if g or i:
                where = {"groups": lax.rem(group + g, groups), "inst": lax.rem(me + i, insts)}
                peers.append(where)

    barrier = pltpu.get_barrier_semaphore()
    for where in peers:
        pl.semaphore_signal(barrier, inc=1, device_id=where, device_id_type=MESH_ID)
    pl.semaphore_wait(barrier, len(peers))

    def remote(src, dst, send, recv, where):
        return pltpu.make_async_remote_copy(
            src_ref=src, dst_ref=dst, send_sem=send, recv_sem=recv,
            device_id=where, device_id_type=MESH_ID,
        )

    def place(inst):
        return first_ref.at[pl.ds(inst * blocks, blocks)]

    here = group * insts + me
    plans = [
        remote(plan_ref, every_ref.at[here], plan_send.at[i], plan_recv.at[i], where)
        for i, where in enumerate(peers)
    ]
    source = prompt_ref.at[:, pl.ds(0, rows), :]
    crossing = [
        remote(
            source, place(me), x_send.at[s - 1], x_recv.at[s - 1],
            {"inst": lax.rem(chip + s, chips) * CORES + core},
        )
        for s in range(1, chips)
    ]
    own = remote(source, place(me), own_send.at[0], own_recv.at[0], {"inst": partner})
    kept = pltpu.make_async_copy(source, place(me), local_sem.at[0])
    plan_kept = pltpu.make_async_copy(plan_ref, every_ref.at[here], local_sem.at[1])
    for copy in plans + crossing + [own, kept, plan_kept]:
        copy.start()
    hops = []
    for s in range(1, chips):
        crossing[s - 1].wait_recv()
        part = place(lax.rem(chip + chips - s, chips) * CORES + core)
        hops.append(remote(part, part, hop_send.at[s - 1], hop_recv.at[s - 1], {"inst": partner}))
        hops[-1].start()
    kept.wait()
    plan_kept.wait()
    for copy in plans + [own] + hops:
        copy.wait()
    for copy in crossing:
        copy.wait_send()


def opening(plan, prompt, groups, insts, collective_id):
    blocks, rows, width = prompt.shape
    chips = insts // CORES
    peers = groups * insts - 1
    first = rows // sum(PARTS) * PARTS[0]
    dma = pltpu.SemaphoreType.DMA
    return pl.pallas_call(
        functools.partial(opening_kernel, groups, insts),
        out_shape=[
            jax.ShapeDtypeStruct((groups * insts,) + plan.shape, plan.dtype),
            jax.ShapeDtypeStruct((insts * blocks, first, width), prompt.dtype),
        ],
        in_specs=[
            pl.BlockSpec(memory_space=pltpu.VMEM),
            pl.BlockSpec(memory_space=pl.ANY),
        ],
        out_specs=[
            pl.BlockSpec(memory_space=pltpu.VMEM),
            pl.BlockSpec(memory_space=pl.ANY),
        ],
        scratch_shapes=[
            dma((peers,)), dma((peers,)),
            dma((chips - 1,)), dma((chips - 1,)),
            dma((1,)), dma((1,)),
            dma((chips - 1,)), dma((chips - 1,)),
            dma((2,)),
        ],
        compiler_params=pltpu.CompilerParams(
            collective_id=collective_id, has_side_effects=True, vmem_limit_bytes=48 * MIB
        ),
        name="opening",
    )(plan, prompt)


def migrate_kernel(
    insts, tps, share, sent, index_ref, prompt_ref, first_ref, page_ref, packed,
    x_send, x_recv, own_send, own_recv, hop_send, hop_recv,
    z_send, z_recv, back_send, back_recv, local_sem, keep_sem, *gathered,
):
    me = lax.axis_index("inst")
    tp = lax.axis_index("tp")
    core = lax.rem(me, CORES)
    chip = me // CORES
    chips = insts // CORES
    partner = me + 1 - 2 * core
    blocks, rows, width = prompt_ref.shape
    unit = rows // sum(PARTS)

    def mirror(step):
        return lax.rem(chip + step, chips) * CORES + core

    def tp_peer(step):
        return lax.rem(tp + step, tps)

    barrier = pltpu.get_barrier_semaphore()
    pl.semaphore_signal(barrier, inc=1, device_id={"inst": partner}, device_id_type=MESH_ID)
    for step in range(1, chips):
        pl.semaphore_signal(barrier, inc=1, device_id={"inst": mirror(step)}, device_id_type=MESH_ID)
    for step in range(1, tps):
        pl.semaphore_signal(barrier, inc=1, device_id={"tp": tp_peer(step)}, device_id_type=MESH_ID)
    pl.semaphore_wait(barrier, chips + tps - 1)

    def span(c):
        return pl.ds(sum(PARTS[:c]) * unit, PARTS[c] * unit)

    def remote(src, dst, send, recv, where):
        return pltpu.make_async_remote_copy(
            src_ref=src, dst_ref=dst, send_sem=send, recv_sem=recv,
            device_id=where, device_id_type=MESH_ID,
        )

    def place(inst):
        return pl.ds(inst * blocks, blocks)

    def cross(c):
        src = prompt_ref.at[:, span(c), :]
        dst = gathered[c].at[place(me)]
        return [
            remote(src, dst, x_send.at[c, s - 1], x_recv.at[c, s - 1], {"inst": mirror(s)})
            for s in range(1, chips)
        ]

    def own(c):
        src = prompt_ref.at[:, span(c), :]
        dst = gathered[c].at[place(me)]
        return (
            remote(src, dst, own_send.at[c], own_recv.at[c], {"inst": partner}),
            pltpu.make_async_copy(src, dst, local_sem.at[c]),
        )

    def hop(c, s):
        origin = lax.rem(chip + chips - s, chips) * CORES + core
        part = gathered[c].at[place(origin)]
        return remote(part, part, hop_send.at[c, s - 1], hop_recv.at[c, s - 1], {"inst": partner})

    def spread(c):
        copies = []
        dst = page_ref.at[
            pl.ds(core * share, sent), span(c), pl.ds(pl.multiple_of(tp * width, 128), width)
        ]
        for s in range(1, tps):
            peer = tp_peer(s)
            src = packed.at[pl.ds(peer * sent, sent), span(c), :]
            copies.append(
                remote(src, dst, z_send.at[c, s - 1], z_recv.at[c, s - 1], {"tp": peer})
            )
        kept = packed.at[pl.ds(tp * sent, sent), span(c), :]
        return copies, pltpu.make_async_copy(kept, dst, keep_sem.at[c])

    def back(c):
        part = page_ref.at[pl.ds(core * share, sent), span(c), :]
        return remote(part, part, back_send.at[c], back_recv.at[c], {"inst": partner})

    def begin(c):
        for copy in cross(c):
            copy.start()
        for copy in own(c):
            copy.start()

    def finish_spread(c):
        copies, kept = spread(c)
        for copy in copies:
            copy.wait_recv()
        kept.wait()
        back(c).start()

    first = pltpu.make_async_copy(first_ref, gathered[0], local_sem.at[0])
    first.start()
    begin(1)
    begin(2)
    for c in range(PIECES):
        if c and c + 2 < PIECES:
            begin(c + 2)
        if c:
            crossing = cross(c)
            for s in range(1, chips):
                crossing[s - 1].wait_recv()
                hop(c, s).start()
            to_partner, kept = own(c)
            kept.wait()
            to_partner.wait_recv()
            for s in range(1, chips):
                hop(c, s).wait_recv()
        else:
            first.wait()

        def pack(entry, carry):
            chosen = index_ref[entry // sent * share + lax.rem(entry, sent)]
            packed[entry, span(c), :] = gathered[c][chosen]
            return carry

        lax.fori_loop(0, tps * sent, pack, 0, unroll=4)
        copies, kept = spread(c)
        for copy in copies:
            copy.start()
        kept.start()
        if c >= 1:
            finish_spread(c - 1)
    finish_spread(PIECES - 1)
    for c in range(PIECES):
        if c:
            for copy in cross(c):
                copy.wait_send()
            own(c)[0].wait_send()
            for s in range(1, chips):
                hop(c, s).wait_send()
        for copy in spread(c)[0]:
            copy.wait_send()
        back(c).wait()


def migrate(insts, tps, share, sent, collective_id, index, prompt, first):
    blocks, rows, width = prompt.shape
    chips = insts // CORES
    dma = pltpu.SemaphoreType.DMA
    return pl.pallas_call(
        functools.partial(migrate_kernel, insts, tps, share, sent),
        out_shape=jax.ShapeDtypeStruct((CORES * share, rows, width * tps), prompt.dtype),
        in_specs=[
            pl.BlockSpec(memory_space=pltpu.SMEM),
            pl.BlockSpec(memory_space=pl.ANY),
            pl.BlockSpec(memory_space=pl.ANY),
        ],
        out_specs=pl.BlockSpec(memory_space=pl.ANY),
        scratch_shapes=[
            pltpu.VMEM((tps * sent, rows, width), prompt.dtype),
            dma((PIECES, chips - 1)), dma((PIECES, chips - 1)),
            dma((PIECES,)), dma((PIECES,)),
            dma((PIECES, chips - 1)), dma((PIECES, chips - 1)),
            dma((PIECES, tps - 1)), dma((PIECES, tps - 1)),
            dma((PIECES,)), dma((PIECES,)),
            dma((PIECES,)), dma((PIECES,)),
        ]
        + [
            pltpu.VMEM((insts * blocks, rows // sum(PARTS) * part, width), prompt.dtype)
            for part in PARTS
        ],
        compiler_params=pltpu.CompilerParams(
            collective_id=collective_id, has_side_effects=True, vmem_limit_bytes=48 * MIB
        ),
        name=f"migrate_{sent}",
    )(index, prompt, first)


def attend_kernel(page_local, flag_ref, place_ref, kept_ref, length_ref, base_ref, *refs):
    pages, residents = refs[:PAGES_STEP], refs[PAGES_STEP : 2 * PAGES_STEP]
    query_ref, out_ref, numerator_ref, stat_ref, peak_ref, denominator_ref = refs[2 * PAGES_STEP :]
    step = pl.program_id(0)
    seq = step * PAGES_STEP // page_local
    first = lax.rem(step * PAGES_STEP, page_local)

    for i in range(PAGES_STEP):
        fresh = flag_ref[step * PAGES_STEP + i] > 0

        @pl.when(fresh)
        def _():
            out_ref[i] = pages[i][0]

        @pl.when(jnp.logical_not(fresh))
        def _():
            out_ref[i] = residents[i][0]

    @pl.when(first == 0)
    def _():
        peak_ref[...] = jnp.full(peak_ref.shape, masked_score, jnp.float32)
        denominator_ref[...] = jnp.zeros(denominator_ref.shape, jnp.float32)
        numerator_ref[...] = jnp.zeros(numerator_ref.shape, jnp.float32)

    tokens = out_ref.shape[1] // 2
    scores = jnp.concatenate(
        [
            lax.dot_general(
                query_ref[0],
                out_ref[i, :tokens, :],
                (((1,), (1,)), ((), ())),
                preferred_element_type=jnp.float32,
            )
            for i in range(PAGES_STEP)
        ],
        axis=1,
    ) * HD ** (-0.5)
    row = lax.broadcasted_iota(jnp.int32, scores.shape, 0)
    start = base_ref[0] + first * tokens
    position = start + lax.broadcasted_iota(jnp.int32, scores.shape, 1)
    decode_step = lax.rem(row // GROUP, STEPS)
    limit = jnp.full(scores.shape, length_ref[seq * STEPS], jnp.int32)
    for e in range(1, STEPS):
        limit = jnp.where(decode_step == e, length_ref[seq * STEPS + e], limit)
    usable = position < limit
    old_peak = peak_ref[...]
    best = jnp.max(jnp.where(usable, scores, masked_score), axis=1, keepdims=True)
    peak = jnp.maximum(old_peak, best)
    factor = jnp.exp(old_peak - peak)
    weights = jnp.where(usable, jnp.exp(scores - peak[:, :1]), 0.0)
    denominator = denominator_ref[...] * factor + jnp.sum(weights, axis=1, keepdims=True)
    peak_ref[...] = peak
    denominator_ref[...] = denominator
    high = weights.astype(jnp.bfloat16)
    low = (weights - high.astype(jnp.float32)).astype(jnp.bfloat16)
    rows = STEPS * GROUP
    for v in range(KVH):
        part = slice(v * rows, (v + 1) * rows)
        both = jnp.concatenate([high[part], low[part]], axis=0)
        product = sum(
            jnp.dot(
                both[:, i * tokens : (i + 1) * tokens],
                out_ref[i, tokens:, v * HD : (v + 1) * HD],
                preferred_element_type=jnp.float32,
            )
            for i in range(PAGES_STEP)
        )
        numerator_ref[0, part, :] = (
            numerator_ref[0, part, :] * factor[part] + product[:rows] + product[rows:]
        )

    @pl.when(first == page_local - PAGES_STEP)
    def _():
        lane = lax.broadcasted_iota(jnp.int32, stat_ref.shape, 1)
        spot = lane // (LANES // 4)
        stats = jnp.where(spot == 2 * seq, peak, stat_ref[...])
        stat_ref[...] = jnp.where(spot == 2 * seq + 1, denominator, stats)


def attend(flags, places, kept, lengths, base, pages, resident, queries, seqs):
    total, rows, width = resident.shape
    page_local = total // seqs
    heads = KVH * STEPS * GROUP
    steps_seq = page_local // PAGES_STEP

    def page_spec(which, i):
        return pl.BlockSpec(
            (1, rows, width), lambda s, *scalars: (scalars[which][s * PAGES_STEP + i], 0, 0)
        )

    grid_spec = pltpu.PrefetchScalarGridSpec(
        num_scalar_prefetch=5,
        grid=(total // PAGES_STEP,),
        in_specs=[page_spec(1, i) for i in range(PAGES_STEP)]
        + [page_spec(2, i) for i in range(PAGES_STEP)]
        + [pl.BlockSpec((1, heads, KVH * HD), lambda s, *scalars: (s // steps_seq, 0, 0))],
        out_specs=[
            pl.BlockSpec((PAGES_STEP, rows, width), lambda s, *scalars: (s, 0, 0)),
            pl.BlockSpec((1, heads, HD), lambda s, *scalars: (s // steps_seq, 0, 0)),
            pl.BlockSpec((heads, LANES), lambda s, *scalars: (0, 0)),
        ],
        scratch_shapes=[pltpu.VMEM((heads, LANES), jnp.float32)] * 2,
    )
    return pl.pallas_call(
        functools.partial(attend_kernel, page_local),
        grid_spec=grid_spec,
        out_shape=[
            jax.ShapeDtypeStruct(resident.shape, resident.dtype),
            jax.ShapeDtypeStruct((seqs, heads, HD), jnp.float32),
            jax.ShapeDtypeStruct((heads, LANES), jnp.float32),
        ],
        compiler_params=pltpu.CompilerParams(vmem_limit_bytes=58 * MIB),
        name="attend",
    )(
        flags, places, kept, lengths, base,
        *[pages] * PAGES_STEP, *[resident] * PAGES_STEP, queries,
    )


def combine_kernel(tps, numerator_ref, stat_ref, out_ref, held, held_stat, send_sem, recv_sem, local_sem):
    tp = lax.axis_index("tp")
    seqs, rows = out_ref.shape[:2]
    barrier = pltpu.get_barrier_semaphore()
    for s in range(1, tps):
        pl.semaphore_signal(
            barrier, inc=1, device_id={"tp": lax.rem(tp + s, tps)}, device_id_type=MESH_ID
        )
    pl.semaphore_wait(barrier, tps - 1)
    copies = []
    for s in range(1, tps):
        peer = lax.rem(tp + s, tps)
        part = pl.ds(pl.multiple_of(peer * rows, 8), rows)
        for kind, (src, dst) in enumerate(
            ((numerator_ref.at[:, part, :], held), (stat_ref.at[part, :], held_stat))
        ):
            copies.append(
                pltpu.make_async_remote_copy(
                    src_ref=src,
                    dst_ref=dst.at[s],
                    send_sem=send_sem.at[kind, s - 1],
                    recv_sem=recv_sem.at[kind, s - 1],
                    device_id={"tp": peer},
                    device_id_type=MESH_ID,
                )
            )
    for copy in copies:
        copy.start()
    mine = pl.ds(pl.multiple_of(tp * rows, 8), rows)
    step = LANES // 4
    copies.append(
        pltpu.make_async_copy(numerator_ref.at[:, mine, :], held.at[0], local_sem.at[0])
    )
    copies.append(pltpu.make_async_copy(stat_ref.at[mine, :], held_stat.at[0], local_sem.at[1]))
    for copy in copies[-2:]:
        copy.start()
    for copy in copies:
        copy.wait()
    for seq in range(seqs):
        stats = [held_stat[s] for s in range(tps)]
        tops = [held[s, seq] for s in range(tps)]
        peaks = [part[:, 2 * seq * step : 2 * seq * step + 1] for part in stats]
        lows = [part[:, (2 * seq + 1) * step : (2 * seq + 1) * step + 1] for part in stats]
        peak = functools.reduce(jnp.maximum, peaks)
        factors = [jnp.exp(part - peak) for part in peaks]
        numerator = sum(top * factor for top, factor in zip(tops, factors))
        denominator = sum(low * factor for low, factor in zip(lows, factors))
        out_ref[seq] = (numerator / denominator).astype(out_ref.dtype)


def combine(numerator, stats, tps, collective_id):
    seqs, heads, size = numerator.shape
    rows = heads // tps
    return pl.pallas_call(
        functools.partial(combine_kernel, tps),
        out_shape=jax.ShapeDtypeStruct((seqs, rows, size), jnp.bfloat16),
        in_specs=[pl.BlockSpec(memory_space=pl.ANY)] * 2,
        out_specs=pl.BlockSpec(memory_space=pltpu.VMEM),
        scratch_shapes=[
            pltpu.VMEM((tps, seqs, rows, size), jnp.float32),
            pltpu.VMEM((tps, rows, LANES), jnp.float32),
            pltpu.SemaphoreType.DMA((2, tps - 1)),
            pltpu.SemaphoreType.DMA((2, tps - 1)),
            pltpu.SemaphoreType.DMA((2,)),
        ],
        compiler_params=pltpu.CompilerParams(collective_id=collective_id, has_side_effects=True),
        name="combine",
    )(numerator, stats)


def on_device(prompt_blocks, block_dest, block_slot, resident_cache, queries, context_length):
    insts = lax.axis_size("inst")
    tps = lax.axis_size("tp")
    me = lax.axis_index("inst")
    tp = lax.axis_index("tp")
    blocks, kinds, tokens, width = prompt_blocks.shape
    seqs, page_local = resident_cache.shape[:2]
    pages_seq = page_local * tps
    share = seqs * page_local
    prompt = prompt_blocks.reshape(blocks, kinds * tokens, width)
    plan = jnp.concatenate([block_dest, block_slot])
    plan = jnp.pad(plan[None, :], ((0, 7), (0, -plan.shape[0] % LANES)))
    groups = lax.axis_size("groups")
    plans, first = opening(plan, prompt, groups, insts, len(LEVELS) + 1)
    pairs = plans[:, 0, : 2 * blocks].reshape(groups, insts, 2, blocks).transpose(0, 2, 1, 3)
    pairs = pairs.reshape(groups, 2, insts * blocks)
    load = pairs[:, 0] // CORES * tps + pairs[:, 1] % pages_seq // page_local
    pools = jnp.arange(insts // CORES * tps, dtype=jnp.int32)
    counts = jnp.sum(load[:, :, None] == pools, axis=1, dtype=jnp.int32)
    needed = (jnp.max(counts) + CORES - 1) // CORES
    every = lax.dynamic_index_in_dim(pairs, lax.axis_index("groups"), 0, keepdims=False)
    dest, slot = every[0], every[1]
    total = insts * blocks
    holder = (slot % pages_seq) // page_local
    pool = (dest // CORES) * tps + holder
    order = jnp.arange(total, dtype=jnp.int32)
    rank = jnp.sum(
        jnp.logical_and(pool[:, None] == pool[None, :], order[None, :] < order[:, None]),
        axis=1,
        dtype=jnp.int32,
    )
    entry = jnp.arange(tps * share, dtype=jnp.int32)
    entry_pool = (me // CORES) * tps + entry // share
    entry_rank = (entry % share) * CORES + me % CORES
    hits = jnp.logical_and(pool[None, :] == entry_pool[:, None], rank[None, :] == entry_rank[:, None])
    index = jnp.sum(jnp.where(hits, order[None, :], 0), axis=1, dtype=jnp.int32)
    local = jnp.arange(share, dtype=jnp.int32)
    wanted = (local // page_local) * pages_seq + tp * page_local + local % page_local
    found = jnp.logical_and(dest[None, :] == me, slot[None, :] == wanted[:, None])
    spot = (rank % CORES) * share + rank // CORES
    places = jnp.sum(jnp.where(found, spot[None, :], 0), axis=1, dtype=jnp.int32)
    flags = jnp.any(found, axis=1).astype(jnp.int32)

    levels = sorted({-(-share * level // LEVELS[-1]) for level in LEVELS})
    variant = sum((needed > level).astype(jnp.int32) for level in levels[:-1])
    pages = lax.switch(
        variant,
        [
            functools.partial(migrate, insts, tps, share, sent, i)
            for i, sent in enumerate(levels)
        ],
        index,
        prompt,
        first,
    )
    place_rows, kept_rows = [], []
    place_now = kept_now = jnp.zeros((PAGES_STEP,), jnp.int32)
    for row in range(share // PAGES_STEP):
        part = slice(row * PAGES_STEP, (row + 1) * PAGES_STEP)
        fresh = flags[part] > 0
        place_now = jnp.where(fresh, places[part], place_now)
        kept_now = jnp.where(fresh, kept_now, local[part])
        place_rows.append(place_now)
        kept_rows.append(kept_now)
    places, kept = jnp.concatenate(place_rows), jnp.concatenate(kept_rows)

    by_head = queries.reshape(seqs, STEPS, KVH, GROUP, HD).transpose(0, 2, 1, 3, 4)
    by_head = by_head.reshape(seqs, KVH, STEPS * GROUP, 1, HD)
    diagonal = jnp.eye(KVH, dtype=jnp.bool_)[None, :, None, :, None]
    wide = jnp.where(diagonal, by_head, jnp.zeros((), queries.dtype))
    wide = wide.reshape(seqs, KVH * STEPS * GROUP, KVH * HD)
    base = (tp * pages_seq // tps * tokens).astype(jnp.int32).reshape(1)
    resident = resident_cache.reshape(share, kinds * tokens, width * tps)
    installed, numerator, stats = attend(
        flags, places, kept, context_length, base, pages, resident, wide, seqs
    )
    merged = combine(numerator, stats, tps, len(LEVELS))
    attended = merged.reshape(seqs, KVH // tps, STEPS, GROUP, HD).transpose(0, 2, 1, 3, 4)
    attended = attended.reshape(seqs * STEPS, H * HD // tps)
    return attended, installed.reshape(resident_cache.shape)


def solution(mesh):
    in_specs = (
        P(("groups", "inst"), None, None, "tp"),
        P(("groups", "inst")),
        P(("groups", "inst")),
        P(("groups", "inst"), "tp", None, None, None),
        P(("groups", "inst"), None),
        P(("groups", "inst")),
    )
    out_specs = (P(("groups", "inst"), "tp"), P(("groups", "inst"), "tp", None, None, None))
    return jax.shard_map(
        on_device, mesh=mesh, in_specs=in_specs, out_specs=out_specs, check_vma=False
    )
```

```python
import functools

import jax
import jax.numpy as jnp
from jax import lax
from jax.experimental import pallas as pl
from jax.experimental.pallas import tpu as pltpu
from jax.sharding import PartitionSpec as P

H = 64
KVH = 8
HD = 128
STEPS = 2
GROUP = H // KVH
CORES = 2
PARTS = (1,) * 16
PIECES = len(PARTS)
LEVELS = (10, 11, 12, 16)
SPILL = 2
AHEAD = 5
PAGES_STEP = 4
LANES = 128
MIB = 1024 * 1024

masked_score = -1e30
MESH_ID = pl.DeviceIdType.MESH


def opening_kernel(
    groups, insts, plan_ref, prompt_ref, every_ref, first_ref,
    plan_send, plan_recv, x_send, x_recv, own_send, own_recv, hop_send, hop_recv, local_sem,
):
    group = lax.axis_index("groups")
    me = lax.axis_index("inst")
    core = lax.rem(me, CORES)
    chip = me // CORES
    chips = insts // CORES
    partner = me + 1 - 2 * core
    blocks = prompt_ref.shape[0]
    rows = first_ref.shape[1]
    peers = []
    for g in range(groups):
        for i in range(insts):
            if g or i:
                where = {"groups": lax.rem(group + g, groups), "inst": lax.rem(me + i, insts)}
                peers.append(where)

    barrier = pltpu.get_barrier_semaphore()
    for where in peers:
        pl.semaphore_signal(barrier, inc=1, device_id=where, device_id_type=MESH_ID)
    pl.semaphore_wait(barrier, len(peers))

    def remote(src, dst, send, recv, where):
        return pltpu.make_async_remote_copy(
            src_ref=src, dst_ref=dst, send_sem=send, recv_sem=recv,
            device_id=where, device_id_type=MESH_ID,
        )

    def place(inst):
        return first_ref.at[pl.ds(inst * blocks, blocks)]

    here = group * insts + me
    plans = [
        remote(plan_ref, every_ref.at[here], plan_send.at[i], plan_recv.at[i], where)
        for i, where in enumerate(peers)
    ]
    source = prompt_ref.at[:, pl.ds(0, rows), :]
    crossing = [
        remote(
            source, place(me), x_send.at[s - 1], x_recv.at[s - 1],
            {"inst": lax.rem(chip + s, chips) * CORES + core},
        )
        for s in range(1, chips)
    ]
    own = remote(source, place(me), own_send.at[0], own_recv.at[0], {"inst": partner})
    kept = pltpu.make_async_copy(source, place(me), local_sem.at[0])
    plan_kept = pltpu.make_async_copy(plan_ref, every_ref.at[here], local_sem.at[1])
    for copy in plans + crossing + [own, kept, plan_kept]:
        copy.start()
    hops = []
    for s in range(1, chips):
        crossing[s - 1].wait_recv()
        part = place(lax.rem(chip + chips - s, chips) * CORES + core)
        hops.append(remote(part, part, hop_send.at[s - 1], hop_recv.at[s - 1], {"inst": partner}))
        hops[-1].start()
    kept.wait()
    plan_kept.wait()
    for copy in plans + [own] + hops:
        copy.wait()
    for copy in crossing:
        copy.wait_send()


def opening(plan, prompt, groups, insts, collective_id):
    blocks, rows, width = prompt.shape
    chips = insts // CORES
    peers = groups * insts - 1
    first = rows // sum(PARTS) * PARTS[0]
    dma = pltpu.SemaphoreType.DMA
    return pl.pallas_call(
        functools.partial(opening_kernel, groups, insts),
        out_shape=[
            jax.ShapeDtypeStruct((groups * insts,) + plan.shape, plan.dtype),
            jax.ShapeDtypeStruct((insts * blocks, first, width), prompt.dtype),
        ],
        in_specs=[
            pl.BlockSpec(memory_space=pltpu.VMEM),
            pl.BlockSpec(memory_space=pl.ANY),
        ],
        out_specs=[
            pl.BlockSpec(memory_space=pltpu.VMEM),
            pl.BlockSpec(memory_space=pl.ANY),
        ],
        scratch_shapes=[
            dma((peers,)), dma((peers,)),
            dma((chips - 1,)), dma((chips - 1,)),
            dma((1,)), dma((1,)),
            dma((chips - 1,)), dma((chips - 1,)),
            dma((2,)),
        ],
        compiler_params=pltpu.CompilerParams(
            collective_id=collective_id, has_side_effects=True, vmem_limit_bytes=48 * MIB
        ),
        name="opening",
    )(plan, prompt)


def migrate_kernel(
    insts, tps, share, sent, spill, index_ref, prompt_ref, first_ref, page_ref, packed,
    x_send, x_recv, own_send, own_recv, hop_send, hop_recv,
    z_send, z_recv, back_send, back_recv, home_send, home_recv, pass_send, pass_recv,
    local_sem, keep_sem, *gathered,
):
    me = lax.axis_index("inst")
    tp = lax.axis_index("tp")
    core = lax.rem(me, CORES)
    chip = me // CORES
    chips = insts // CORES
    partner = me + 1 - 2 * core
    blocks, rows, width = prompt_ref.shape
    unit = rows // sum(PARTS)

    def mirror(step):
        return lax.rem(chip + step, chips) * CORES + core

    def tp_peer(step):
        return lax.rem(tp + step, tps)

    barrier = pltpu.get_barrier_semaphore()
    pl.semaphore_signal(barrier, inc=1, device_id={"inst": partner}, device_id_type=MESH_ID)
    for step in range(1, chips):
        pl.semaphore_signal(barrier, inc=1, device_id={"inst": mirror(step)}, device_id_type=MESH_ID)
    for step in range(1, tps):
        pl.semaphore_signal(barrier, inc=1, device_id={"tp": tp_peer(step)}, device_id_type=MESH_ID)
    pl.semaphore_wait(barrier, chips + tps - 1)

    def span(c):
        return pl.ds(sum(PARTS[:c]) * unit, PARTS[c] * unit)

    def remote(src, dst, send, recv, where):
        return pltpu.make_async_remote_copy(
            src_ref=src, dst_ref=dst, send_sem=send, recv_sem=recv,
            device_id=where, device_id_type=MESH_ID,
        )

    def place(inst):
        return pl.ds(inst * blocks, blocks)

    def cross(c):
        src = prompt_ref.at[:, span(c), :]
        dst = gathered[c].at[place(me)]
        return [
            remote(src, dst, x_send.at[c, s - 1], x_recv.at[c, s - 1], {"inst": mirror(s)})
            for s in range(1, chips)
        ]

    def own(c):
        src = prompt_ref.at[:, span(c), :]
        dst = gathered[c].at[place(me)]
        return (
            remote(src, dst, own_send.at[c], own_recv.at[c], {"inst": partner}),
            pltpu.make_async_copy(src, dst, local_sem.at[c]),
        )

    def hop(c, s):
        origin = lax.rem(chip + chips - s, chips) * CORES + core
        part = gathered[c].at[place(origin)]
        return remote(part, part, hop_send.at[c, s - 1], hop_recv.at[c, s - 1], {"inst": partner})

    def spread(c):
        copies = []
        dst = page_ref.at[
            pl.ds(core * share, sent), span(c), pl.ds(pl.multiple_of(tp * width, 128), width)
        ]
        for s in range(1, tps):
            peer = tp_peer(s)
            src = packed.at[pl.ds(peer * sent, sent), span(c), :]
            copies.append(
                remote(src, dst, z_send.at[c, s - 1], z_recv.at[c, s - 1], {"tp": peer})
            )
        kept = packed.at[pl.ds(tp * sent, sent), span(c), :]
        return copies, pltpu.make_async_copy(kept, dst, keep_sem.at[c])

    def back(c):
        part = page_ref.at[pl.ds(core * share, sent), span(c), :]
        return remote(part, part, back_send.at[c], back_recv.at[c], {"inst": partner})

    def home(c):
        src = page_ref.at[pl.ds(core * share + sent - spill, spill), span(c), :]
        dst = page_ref.at[pl.ds(CORES * share + core * spill, spill), span(c), :]
        return remote(src, dst, home_send.at[c], home_recv.at[c], {"inst": mirror(1)})

    def pass_on(c):
        part = page_ref.at[pl.ds(CORES * share + core * spill, spill), span(c), :]
        return remote(part, part, pass_send.at[c], pass_recv.at[c], {"inst": partner})

    def begin(c):
        for copy in cross(c):
            copy.start()
        for copy in own(c):
            copy.start()

    def finish_spread(c):
        copies, kept = spread(c)
        for copy in copies:
            copy.wait_recv()
        kept.wait()
        back(c).start()
        if spill:
            home(c).start()

    def finish_home(c):
        if spill:
            home(c).wait_recv()
            pass_on(c).start()

    first = pltpu.make_async_copy(first_ref, gathered[0], local_sem.at[0])
    first.start()
    for c in range(1, AHEAD):
        begin(c)
    for c in range(PIECES):
        if c and c + AHEAD - 1 < PIECES:
            begin(c + AHEAD - 1)
        if c:
            crossing = cross(c)
            for s in range(1, chips):
                crossing[s - 1].wait_recv()
                hop(c, s).start()
            to_partner, kept = own(c)
            kept.wait()
            to_partner.wait_recv()
            for s in range(1, chips):
                hop(c, s).wait_recv()
        else:
            first.wait()

        def pack(entry, carry):
            chosen = index_ref[entry // sent * share + lax.rem(entry, sent)]
            packed[entry, span(c), :] = gathered[c][chosen]
            return carry

        lax.fori_loop(0, tps * sent, pack, 0, unroll=4)
        copies, kept = spread(c)
        for copy in copies:
            copy.start()
        kept.start()
        if c >= 1:
            finish_spread(c - 1)
        if c >= 2:
            finish_home(c - 2)
    finish_spread(PIECES - 1)
    finish_home(PIECES - 2)
    finish_home(PIECES - 1)
    for c in range(PIECES):
        if c:
            for copy in cross(c):
                copy.wait_send()
            own(c)[0].wait_send()
            for s in range(1, chips):
                hop(c, s).wait_send()
        for copy in spread(c)[0]:
            copy.wait_send()
        back(c).wait()
        if spill:
            home(c).wait_send()
            pass_on(c).wait()


def migrate(insts, tps, share, sent, spill, collective_id, index, prompt, first):
    blocks, rows, width = prompt.shape
    chips = insts // CORES
    dma = pltpu.SemaphoreType.DMA
    return pl.pallas_call(
        functools.partial(migrate_kernel, insts, tps, share, sent, spill),
        out_shape=jax.ShapeDtypeStruct(
            (CORES * (share + SPILL), rows, width * tps), prompt.dtype
        ),
        in_specs=[
            pl.BlockSpec(memory_space=pltpu.SMEM),
            pl.BlockSpec(memory_space=pl.ANY),
            pl.BlockSpec(memory_space=pl.ANY),
        ],
        out_specs=pl.BlockSpec(memory_space=pl.ANY),
        scratch_shapes=[
            pltpu.VMEM((tps * sent, rows, width), prompt.dtype),
            dma((PIECES, chips - 1)), dma((PIECES, chips - 1)),
            dma((PIECES,)), dma((PIECES,)),
            dma((PIECES, chips - 1)), dma((PIECES, chips - 1)),
            dma((PIECES, tps - 1)), dma((PIECES, tps - 1)),
            dma((PIECES,)), dma((PIECES,)),
            dma((PIECES,)), dma((PIECES,)),
            dma((PIECES,)), dma((PIECES,)),
            dma((PIECES,)), dma((PIECES,)),
        ]
        + [
            pltpu.VMEM((insts * blocks, rows // sum(PARTS) * part, width), prompt.dtype)
            for part in PARTS
        ],
        compiler_params=pltpu.CompilerParams(
            collective_id=collective_id, has_side_effects=True, vmem_limit_bytes=48 * MIB
        ),
        name=f"migrate_{sent}",
    )(index, prompt, first)


def attend_kernel(page_local, flag_ref, place_ref, kept_ref, length_ref, base_ref, *refs):
    pages, residents = refs[:PAGES_STEP], refs[PAGES_STEP : 2 * PAGES_STEP]
    query_ref, out_ref, numerator_ref, stat_ref, peak_ref, denominator_ref = refs[2 * PAGES_STEP :]
    step = pl.program_id(0)
    seq = step * PAGES_STEP // page_local
    first = lax.rem(step * PAGES_STEP, page_local)

    for i in range(PAGES_STEP):
        fresh = flag_ref[step * PAGES_STEP + i] > 0

        @pl.when(fresh)
        def _():
            out_ref[i] = pages[i][0]

        @pl.when(jnp.logical_not(fresh))
        def _():
            out_ref[i] = residents[i][0]

    @pl.when(first == 0)
    def _():
        peak_ref[...] = jnp.full(peak_ref.shape, masked_score, jnp.float32)
        denominator_ref[...] = jnp.zeros(denominator_ref.shape, jnp.float32)
        numerator_ref[...] = jnp.zeros(numerator_ref.shape, jnp.float32)

    tokens = out_ref.shape[1] // 2
    scores = jnp.concatenate(
        [
            lax.dot_general(
                query_ref[0],
                out_ref[i, :tokens, :],
                (((1,), (1,)), ((), ())),
                preferred_element_type=jnp.float32,
            )
            for i in range(PAGES_STEP)
        ],
        axis=1,
    ) * HD ** (-0.5)
    row = lax.broadcasted_iota(jnp.int32, scores.shape, 0)
    start = base_ref[0] + first * tokens
    position = start + lax.broadcasted_iota(jnp.int32, scores.shape, 1)
    decode_step = lax.rem(row // GROUP, STEPS)
    limit = jnp.full(scores.shape, length_ref[seq * STEPS], jnp.int32)
    for e in range(1, STEPS):
        limit = jnp.where(decode_step == e, length_ref[seq * STEPS + e], limit)
    usable = position < limit
    old_peak = peak_ref[...]
    best = jnp.max(jnp.where(usable, scores, masked_score), axis=1, keepdims=True)
    peak = jnp.maximum(old_peak, best)
    factor = jnp.exp(old_peak - peak)
    weights = jnp.where(usable, jnp.exp(scores - peak[:, :1]), 0.0)
    denominator = denominator_ref[...] * factor + jnp.sum(weights, axis=1, keepdims=True)
    peak_ref[...] = peak
    denominator_ref[...] = denominator
    high = weights.astype(jnp.bfloat16)
    low = (weights - high.astype(jnp.float32)).astype(jnp.bfloat16)
    rows = STEPS * GROUP
    for v in range(KVH):
        part = slice(v * rows, (v + 1) * rows)
        both = jnp.concatenate([high[part], low[part]], axis=0)
        product = sum(
            jnp.dot(
                both[:, i * tokens : (i + 1) * tokens],
                out_ref[i, tokens:, v * HD : (v + 1) * HD],
                preferred_element_type=jnp.float32,
            )
            for i in range(PAGES_STEP)
        )
        numerator_ref[0, part, :] = (
            numerator_ref[0, part, :] * factor[part] + product[:rows] + product[rows:]
        )

    @pl.when(first == page_local - PAGES_STEP)
    def _():
        lane = lax.broadcasted_iota(jnp.int32, stat_ref.shape, 1)
        spot = lane // (LANES // 4)
        stats = jnp.where(spot == 2 * seq, peak, stat_ref[...])
        stat_ref[...] = jnp.where(spot == 2 * seq + 1, denominator, stats)


def attend(flags, places, kept, lengths, base, pages, resident, queries, seqs):
    total, rows, width = resident.shape
    page_local = total // seqs
    heads = KVH * STEPS * GROUP
    steps_seq = page_local // PAGES_STEP

    def page_spec(which, i):
        return pl.BlockSpec(
            (1, rows, width), lambda s, *scalars: (scalars[which][s * PAGES_STEP + i], 0, 0)
        )

    grid_spec = pltpu.PrefetchScalarGridSpec(
        num_scalar_prefetch=5,
        grid=(total // PAGES_STEP,),
        in_specs=[page_spec(1, i) for i in range(PAGES_STEP)]
        + [page_spec(2, i) for i in range(PAGES_STEP)]
        + [pl.BlockSpec((1, heads, KVH * HD), lambda s, *scalars: (s // steps_seq, 0, 0))],
        out_specs=[
            pl.BlockSpec((PAGES_STEP, rows, width), lambda s, *scalars: (s, 0, 0)),
            pl.BlockSpec((1, heads, HD), lambda s, *scalars: (s // steps_seq, 0, 0)),
            pl.BlockSpec((heads, LANES), lambda s, *scalars: (0, 0)),
        ],
        scratch_shapes=[pltpu.VMEM((heads, LANES), jnp.float32)] * 2,
    )
    return pl.pallas_call(
        functools.partial(attend_kernel, page_local),
        grid_spec=grid_spec,
        out_shape=[
            jax.ShapeDtypeStruct(resident.shape, resident.dtype),
            jax.ShapeDtypeStruct((seqs, heads, HD), jnp.float32),
            jax.ShapeDtypeStruct((heads, LANES), jnp.float32),
        ],
        compiler_params=pltpu.CompilerParams(vmem_limit_bytes=58 * MIB),
        name="attend",
    )(
        flags, places, kept, lengths, base,
        *[pages] * PAGES_STEP, *[resident] * PAGES_STEP, queries,
    )


def combine_kernel(tps, numerator_ref, stat_ref, out_ref, held, held_stat, send_sem, recv_sem, local_sem):
    tp = lax.axis_index("tp")
    seqs, rows = out_ref.shape[:2]
    barrier = pltpu.get_barrier_semaphore()
    for s in range(1, tps):
        pl.semaphore_signal(
            barrier, inc=1, device_id={"tp": lax.rem(tp + s, tps)}, device_id_type=MESH_ID
        )
    pl.semaphore_wait(barrier, tps - 1)
    copies = []
    for s in range(1, tps):
        peer = lax.rem(tp + s, tps)
        part = pl.ds(pl.multiple_of(peer * rows, 8), rows)
        for kind, (src, dst) in enumerate(
            ((numerator_ref.at[:, part, :], held), (stat_ref.at[part, :], held_stat))
        ):
            copies.append(
                pltpu.make_async_remote_copy(
                    src_ref=src,
                    dst_ref=dst.at[s],
                    send_sem=send_sem.at[kind, s - 1],
                    recv_sem=recv_sem.at[kind, s - 1],
                    device_id={"tp": peer},
                    device_id_type=MESH_ID,
                )
            )
    for copy in copies:
        copy.start()
    mine = pl.ds(pl.multiple_of(tp * rows, 8), rows)
    step = LANES // 4
    copies.append(
        pltpu.make_async_copy(numerator_ref.at[:, mine, :], held.at[0], local_sem.at[0])
    )
    copies.append(pltpu.make_async_copy(stat_ref.at[mine, :], held_stat.at[0], local_sem.at[1]))
    for copy in copies[-2:]:
        copy.start()
    for copy in copies:
        copy.wait()
    for seq in range(seqs):
        stats = [held_stat[s] for s in range(tps)]
        tops = [held[s, seq] for s in range(tps)]
        peaks = [part[:, 2 * seq * step : 2 * seq * step + 1] for part in stats]
        lows = [part[:, (2 * seq + 1) * step : (2 * seq + 1) * step + 1] for part in stats]
        peak = functools.reduce(jnp.maximum, peaks)
        factors = [jnp.exp(part - peak) for part in peaks]
        numerator = sum(top * factor for top, factor in zip(tops, factors))
        denominator = sum(low * factor for low, factor in zip(lows, factors))
        out_ref[seq] = (numerator / denominator).astype(out_ref.dtype)


def combine(numerator, stats, tps, collective_id):
    seqs, heads, size = numerator.shape
    rows = heads // tps
    return pl.pallas_call(
        functools.partial(combine_kernel, tps),
        out_shape=jax.ShapeDtypeStruct((seqs, rows, size), jnp.bfloat16),
        in_specs=[pl.BlockSpec(memory_space=pl.ANY)] * 2,
        out_specs=pl.BlockSpec(memory_space=pltpu.VMEM),
        scratch_shapes=[
            pltpu.VMEM((tps, seqs, rows, size), jnp.float32),
            pltpu.VMEM((tps, rows, LANES), jnp.float32),
            pltpu.SemaphoreType.DMA((2, tps - 1)),
            pltpu.SemaphoreType.DMA((2, tps - 1)),
            pltpu.SemaphoreType.DMA((2,)),
        ],
        compiler_params=pltpu.CompilerParams(collective_id=collective_id, has_side_effects=True),
        name="combine",
    )(numerator, stats)


def on_device(prompt_blocks, block_dest, block_slot, resident_cache, queries, context_length):
    insts = lax.axis_size("inst")
    tps = lax.axis_size("tp")
    me = lax.axis_index("inst")
    tp = lax.axis_index("tp")
    blocks, kinds, tokens, width = prompt_blocks.shape
    seqs, page_local = resident_cache.shape[:2]
    pages_seq = page_local * tps
    share = seqs * page_local
    prompt = prompt_blocks.reshape(blocks, kinds * tokens, width)
    plan = jnp.concatenate([block_dest, block_slot])
    plan = jnp.pad(plan[None, :], ((0, 7), (0, -plan.shape[0] % LANES)))
    groups = lax.axis_size("groups")
    plans, first = opening(plan, prompt, groups, insts, len(LEVELS) + 1)
    pairs = plans[:, 0, : 2 * blocks].reshape(groups, insts, 2, blocks).transpose(0, 2, 1, 3)
    pairs = pairs.reshape(groups, 2, insts * blocks)
    load = pairs[:, 0] // CORES * tps + pairs[:, 1] % pages_seq // page_local
    pools = jnp.arange(insts // CORES * tps, dtype=jnp.int32)
    counts = jnp.sum(load[:, :, None] == pools, axis=1, dtype=jnp.int32)
    counts = counts.reshape(groups, insts // CORES, tps)
    spill = SPILL if insts // CORES == 2 else 0
    sizes = sorted({-(-share * level // LEVELS[-1]) for level in LEVELS})
    levels = [(size, spill if size < share else 0) for size in sizes]
    variant = jnp.int32(len(levels) - 1)
    cap = jnp.int32(share)
    for i in reversed(range(len(levels) - 1)):
        size, extra = levels[i]
        over = jnp.maximum(counts - CORES * size, 0)
        room = CORES * size - jnp.minimum(counts, CORES * size)
        fits = jnp.all(over <= jnp.minimum(CORES * extra, room[:, ::-1]))
        variant = jnp.where(fits, i, variant)
        cap = jnp.where(fits, size, cap)
    every = lax.dynamic_index_in_dim(pairs, lax.axis_index("groups"), 0, keepdims=False)
    dest, slot = every[0], every[1]
    total = insts * blocks
    holder = (slot % pages_seq) // page_local
    pool = (dest // CORES) * tps + holder
    order = jnp.arange(total, dtype=jnp.int32)
    rank = jnp.sum(
        jnp.logical_and(pool[:, None] == pool[None, :], order[None, :] < order[:, None]),
        axis=1,
        dtype=jnp.int32,
    )
    entry = jnp.arange(tps * share, dtype=jnp.int32)
    entry_pool = (me // CORES) * tps + entry // share
    entry_rank = (entry % share) * CORES + me % CORES
    hits = jnp.logical_and(pool[None, :] == entry_pool[:, None], rank[None, :] == entry_rank[:, None])
    limit = CORES * cap
    if spill:
        other_pool = (1 - me // CORES) * tps + entry // share
        spilled = rank[None, :] == 2 * limit - 1 - entry_rank[:, None]
        spilled = jnp.logical_and(spilled, (rank >= limit)[None, :])
        spilled = jnp.logical_and(spilled, pool[None, :] == other_pool[:, None])
        hits = jnp.logical_or(hits, spilled)
    index = jnp.sum(jnp.where(hits, order[None, :], 0), axis=1, dtype=jnp.int32)
    local = jnp.arange(share, dtype=jnp.int32)
    wanted = (local // page_local) * pages_seq + tp * page_local + local % page_local
    found = jnp.logical_and(dest[None, :] == me, slot[None, :] == wanted[:, None])
    spot = (rank % CORES) * share + rank // CORES
    if spill:
        slot_at = 2 * limit - 1 - rank
        spot_home = CORES * share + (slot_at % CORES) * spill + slot_at // CORES - cap + spill
        spot = jnp.where(rank >= limit, spot_home, spot)
    places = jnp.sum(jnp.where(found, spot[None, :], 0), axis=1, dtype=jnp.int32)
    flags = jnp.any(found, axis=1).astype(jnp.int32)

    pages = lax.switch(
        variant,
        [
            functools.partial(migrate, insts, tps, share, sent, extra, i)
            for i, (sent, extra) in enumerate(levels)
        ],
        index,
        prompt,
        first,
    )
    place_rows, kept_rows = [], []
    place_now = kept_now = jnp.zeros((PAGES_STEP,), jnp.int32)
    for row in range(share // PAGES_STEP):
        part = slice(row * PAGES_STEP, (row + 1) * PAGES_STEP)
        fresh = flags[part] > 0
        place_now = jnp.where(fresh, places[part], place_now)
        kept_now = jnp.where(fresh, kept_now, local[part])
        place_rows.append(place_now)
        kept_rows.append(kept_now)
    places, kept = jnp.concatenate(place_rows), jnp.concatenate(kept_rows)

    by_head = queries.reshape(seqs, STEPS, KVH, GROUP, HD).transpose(0, 2, 1, 3, 4)
    by_head = by_head.reshape(seqs, KVH, STEPS * GROUP, 1, HD)
    diagonal = jnp.eye(KVH, dtype=jnp.bool_)[None, :, None, :, None]
    wide = jnp.where(diagonal, by_head, jnp.zeros((), queries.dtype))
    wide = wide.reshape(seqs, KVH * STEPS * GROUP, KVH * HD)
    base = (tp * pages_seq // tps * tokens).astype(jnp.int32).reshape(1)
    resident = resident_cache.reshape(share, kinds * tokens, width * tps)
    installed, numerator, stats = attend(
        flags, places, kept, context_length, base, pages, resident, wide, seqs
    )
    merged = combine(numerator, stats, tps, len(LEVELS))
    attended = merged.reshape(seqs, KVH // tps, STEPS, GROUP, HD).transpose(0, 2, 1, 3, 4)
    attended = attended.reshape(seqs * STEPS, H * HD // tps)
    return attended, installed.reshape(resident_cache.shape)


def solution(mesh):
    in_specs = (
        P(("groups", "inst"), None, None, "tp"),
        P(("groups", "inst")),
        P(("groups", "inst")),
        P(("groups", "inst"), "tp", None, None, None),
        P(("groups", "inst"), None),
        P(("groups", "inst")),
    )
    out_specs = (P(("groups", "inst"), "tp"), P(("groups", "inst"), "tp", None, None, None))
    return jax.shard_map(
        on_device, mesh=mesh, in_specs=in_specs, out_specs=out_specs, check_vma=False
    )
```

```python
import functools

import jax
import jax.numpy as jnp
from jax import lax
from jax.experimental import pallas as pl
from jax.experimental.pallas import tpu as pltpu
from jax.sharding import PartitionSpec as P

H = 64
KVH = 8
HD = 128
STEPS = 2
GROUP = H // KVH
CORES = 2
PARTS = (1,) * 16
PIECES = len(PARTS)
LEVELS = ((10, 0), (10, 2), (11, 2), (12, 2), (16, 0))
SPILL = 2
AHEAD = 5
HOME_LAG = 6
PAGES_STEP = 4
LANES = 128
MIB = 1024 * 1024

masked_score = -1e30
MESH_ID = pl.DeviceIdType.MESH


def opening_kernel(
    groups, insts, plan_ref, prompt_ref, every_ref, first_ref,
    plan_send, plan_recv, x_send, x_recv, own_send, own_recv, hop_send, hop_recv, local_sem,
):
    group = lax.axis_index("groups")
    me = lax.axis_index("inst")
    core = lax.rem(me, CORES)
    chip = me // CORES
    chips = insts // CORES
    partner = me + 1 - 2 * core
    blocks = prompt_ref.shape[0]
    rows = first_ref.shape[1]
    peers = []
    for g in range(groups):
        for i in range(insts):
            if g or i:
                where = {"groups": lax.rem(group + g, groups), "inst": lax.rem(me + i, insts)}
                peers.append(where)

    barrier = pltpu.get_barrier_semaphore()
    for where in peers:
        pl.semaphore_signal(barrier, inc=1, device_id=where, device_id_type=MESH_ID)
    pl.semaphore_wait(barrier, len(peers))

    def remote(src, dst, send, recv, where):
        return pltpu.make_async_remote_copy(
            src_ref=src, dst_ref=dst, send_sem=send, recv_sem=recv,
            device_id=where, device_id_type=MESH_ID,
        )

    def place(inst):
        return first_ref.at[pl.ds(inst * blocks, blocks)]

    here = group * insts + me
    plans = [
        remote(plan_ref, every_ref.at[here], plan_send.at[i], plan_recv.at[i], where)
        for i, where in enumerate(peers)
    ]
    source = prompt_ref.at[:, pl.ds(0, rows), :]
    crossing = [
        remote(
            source, place(me), x_send.at[s - 1], x_recv.at[s - 1],
            {"inst": lax.rem(chip + s, chips) * CORES + core},
        )
        for s in range(1, chips)
    ]
    own = remote(source, place(me), own_send.at[0], own_recv.at[0], {"inst": partner})
    kept = pltpu.make_async_copy(source, place(me), local_sem.at[0])
    plan_kept = pltpu.make_async_copy(plan_ref, every_ref.at[here], local_sem.at[1])
    for copy in plans + crossing + [own, kept, plan_kept]:
        copy.start()
    hops = []
    for s in range(1, chips):
        crossing[s - 1].wait_recv()
        part = place(lax.rem(chip + chips - s, chips) * CORES + core)
        hops.append(remote(part, part, hop_send.at[s - 1], hop_recv.at[s - 1], {"inst": partner}))
        hops[-1].start()
    kept.wait()
    plan_kept.wait()
    for copy in plans + [own] + hops:
        copy.wait()
    for copy in crossing:
        copy.wait_send()


def opening(plan, prompt, groups, insts, collective_id):
    blocks, rows, width = prompt.shape
    chips = insts // CORES
    peers = groups * insts - 1
    first = rows // sum(PARTS) * PARTS[0]
    dma = pltpu.SemaphoreType.DMA
    return pl.pallas_call(
        functools.partial(opening_kernel, groups, insts),
        out_shape=[
            jax.ShapeDtypeStruct((groups * insts,) + plan.shape, plan.dtype),
            jax.ShapeDtypeStruct((insts * blocks, first, width), prompt.dtype),
        ],
        in_specs=[
            pl.BlockSpec(memory_space=pltpu.VMEM),
            pl.BlockSpec(memory_space=pl.ANY),
        ],
        out_specs=[
            pl.BlockSpec(memory_space=pltpu.VMEM),
            pl.BlockSpec(memory_space=pl.ANY),
        ],
        scratch_shapes=[
            dma((peers,)), dma((peers,)),
            dma((chips - 1,)), dma((chips - 1,)),
            dma((1,)), dma((1,)),
            dma((chips - 1,)), dma((chips - 1,)),
            dma((2,)),
        ],
        compiler_params=pltpu.CompilerParams(
            collective_id=collective_id, has_side_effects=True, vmem_limit_bytes=48 * MIB
        ),
        name="opening",
    )(plan, prompt)


def migrate_kernel(
    insts, tps, share, sent, spill, index_ref, prompt_ref, first_ref, page_ref, packed,
    x_send, x_recv, own_send, own_recv, hop_send, hop_recv,
    z_send, z_recv, back_send, back_recv, home_send, home_recv, pass_send, pass_recv,
    local_sem, keep_sem, *gathered,
):
    me = lax.axis_index("inst")
    tp = lax.axis_index("tp")
    core = lax.rem(me, CORES)
    chip = me // CORES
    chips = insts // CORES
    partner = me + 1 - 2 * core
    blocks, rows, width = prompt_ref.shape
    unit = rows // sum(PARTS)

    def mirror(step):
        return lax.rem(chip + step, chips) * CORES + core

    def tp_peer(step):
        return lax.rem(tp + step, tps)

    barrier = pltpu.get_barrier_semaphore()
    pl.semaphore_signal(barrier, inc=1, device_id={"inst": partner}, device_id_type=MESH_ID)
    for step in range(1, chips):
        pl.semaphore_signal(barrier, inc=1, device_id={"inst": mirror(step)}, device_id_type=MESH_ID)
    for step in range(1, tps):
        pl.semaphore_signal(barrier, inc=1, device_id={"tp": tp_peer(step)}, device_id_type=MESH_ID)
    pl.semaphore_wait(barrier, chips + tps - 1)

    def span(c):
        return pl.ds(sum(PARTS[:c]) * unit, PARTS[c] * unit)

    def remote(src, dst, send, recv, where):
        return pltpu.make_async_remote_copy(
            src_ref=src, dst_ref=dst, send_sem=send, recv_sem=recv,
            device_id=where, device_id_type=MESH_ID,
        )

    def place(inst):
        return pl.ds(inst * blocks, blocks)

    def cross(c):
        src = prompt_ref.at[:, span(c), :]
        dst = gathered[c].at[place(me)]
        return [
            remote(src, dst, x_send.at[c, s - 1], x_recv.at[c, s - 1], {"inst": mirror(s)})
            for s in range(1, chips)
        ]

    def own(c):
        src = prompt_ref.at[:, span(c), :]
        dst = gathered[c].at[place(me)]
        return (
            remote(src, dst, own_send.at[c], own_recv.at[c], {"inst": partner}),
            pltpu.make_async_copy(src, dst, local_sem.at[c]),
        )

    def hop(c, s):
        origin = lax.rem(chip + chips - s, chips) * CORES + core
        part = gathered[c].at[place(origin)]
        return remote(part, part, hop_send.at[c, s - 1], hop_recv.at[c, s - 1], {"inst": partner})

    def spread(c):
        copies = []
        dst = page_ref.at[
            pl.ds(core * share, sent), span(c), pl.ds(pl.multiple_of(tp * width, 128), width)
        ]
        for s in range(1, tps):
            peer = tp_peer(s)
            src = packed.at[pl.ds(peer * sent, sent), span(c), :]
            copies.append(
                remote(src, dst, z_send.at[c, s - 1], z_recv.at[c, s - 1], {"tp": peer})
            )
        kept = packed.at[pl.ds(tp * sent, sent), span(c), :]
        return copies, pltpu.make_async_copy(kept, dst, keep_sem.at[c])

    def back(c):
        part = page_ref.at[pl.ds(core * share, sent), span(c), :]
        return remote(part, part, back_send.at[c], back_recv.at[c], {"inst": partner})

    def home(c):
        src = page_ref.at[pl.ds(core * share + sent - spill, spill), span(c), :]
        dst = page_ref.at[pl.ds(CORES * share + core * spill, spill), span(c), :]
        return remote(src, dst, home_send.at[c], home_recv.at[c], {"inst": mirror(1)})

    def pass_on(c):
        part = page_ref.at[pl.ds(CORES * share + core * spill, spill), span(c), :]
        return remote(part, part, pass_send.at[c], pass_recv.at[c], {"inst": partner})

    def begin(c):
        for copy in cross(c):
            copy.start()
        for copy in own(c):
            copy.start()

    def finish_spread(c):
        copies, kept = spread(c)
        for copy in copies:
            copy.wait_recv()
        kept.wait()
        back(c).start()
        if spill:
            home(c).start()

    def finish_home(c):
        if spill:
            home(c).wait_recv()
            pass_on(c).start()

    first = pltpu.make_async_copy(first_ref, gathered[0], local_sem.at[0])
    first.start()
    for c in range(1, AHEAD):
        begin(c)
    for c in range(PIECES):
        if c and c + AHEAD - 1 < PIECES:
            begin(c + AHEAD - 1)
        if c:
            crossing = cross(c)
            for s in range(1, chips):
                crossing[s - 1].wait_recv()
                hop(c, s).start()
            to_partner, kept = own(c)
            kept.wait()
            to_partner.wait_recv()
            for s in range(1, chips):
                hop(c, s).wait_recv()
        else:
            first.wait()

        def pack(entry, carry):
            chosen = index_ref[entry // sent * share + lax.rem(entry, sent)]
            packed[entry, span(c), :] = gathered[c][chosen]
            return carry

        lax.fori_loop(0, tps * sent, pack, 0, unroll=4)
        copies, kept = spread(c)
        for copy in copies:
            copy.start()
        kept.start()
        if c >= 1:
            finish_spread(c - 1)
        if c >= HOME_LAG:
            finish_home(c - HOME_LAG)
    finish_spread(PIECES - 1)
    for c in range(PIECES - HOME_LAG, PIECES):
        finish_home(c)
    for c in range(PIECES):
        if c:
            for copy in cross(c):
                copy.wait_send()
            own(c)[0].wait_send()
            for s in range(1, chips):
                hop(c, s).wait_send()
        for copy in spread(c)[0]:
            copy.wait_send()
        back(c).wait()
        if spill:
            home(c).wait_send()
            pass_on(c).wait()


def migrate(insts, tps, share, sent, spill, collective_id, index, prompt, first):
    blocks, rows, width = prompt.shape
    chips = insts // CORES
    dma = pltpu.SemaphoreType.DMA
    return pl.pallas_call(
        functools.partial(migrate_kernel, insts, tps, share, sent, spill),
        out_shape=jax.ShapeDtypeStruct(
            (CORES * (share + SPILL), rows, width * tps), prompt.dtype
        ),
        in_specs=[
            pl.BlockSpec(memory_space=pltpu.SMEM),
            pl.BlockSpec(memory_space=pl.ANY),
            pl.BlockSpec(memory_space=pl.ANY),
        ],
        out_specs=pl.BlockSpec(memory_space=pl.ANY),
        scratch_shapes=[
            pltpu.VMEM((tps * sent, rows, width), prompt.dtype),
            dma((PIECES, chips - 1)), dma((PIECES, chips - 1)),
            dma((PIECES,)), dma((PIECES,)),
            dma((PIECES, chips - 1)), dma((PIECES, chips - 1)),
            dma((PIECES, tps - 1)), dma((PIECES, tps - 1)),
            dma((PIECES,)), dma((PIECES,)),
            dma((PIECES,)), dma((PIECES,)),
            dma((PIECES,)), dma((PIECES,)),
            dma((PIECES,)), dma((PIECES,)),
        ]
        + [
            pltpu.VMEM((insts * blocks, rows // sum(PARTS) * part, width), prompt.dtype)
            for part in PARTS
        ],
        compiler_params=pltpu.CompilerParams(
            collective_id=collective_id, has_side_effects=True, vmem_limit_bytes=48 * MIB
        ),
        name=f"migrate_{sent}",
    )(index, prompt, first)


def attend_kernel(page_local, flag_ref, place_ref, kept_ref, length_ref, base_ref, *refs):
    pages, residents = refs[:PAGES_STEP], refs[PAGES_STEP : 2 * PAGES_STEP]
    query_ref, out_ref, numerator_ref, stat_ref, peak_ref, denominator_ref = refs[2 * PAGES_STEP :]
    step = pl.program_id(0)
    seq = step * PAGES_STEP // page_local
    first = lax.rem(step * PAGES_STEP, page_local)

    for i in range(PAGES_STEP):
        fresh = flag_ref[step * PAGES_STEP + i] > 0

        @pl.when(fresh)
        def _():
            out_ref[i] = pages[i][0]

        @pl.when(jnp.logical_not(fresh))
        def _():
            out_ref[i] = residents[i][0]

    @pl.when(first == 0)
    def _():
        peak_ref[...] = jnp.full(peak_ref.shape, masked_score, jnp.float32)
        denominator_ref[...] = jnp.zeros(denominator_ref.shape, jnp.float32)
        numerator_ref[...] = jnp.zeros(numerator_ref.shape, jnp.float32)

    tokens = out_ref.shape[1] // 2
    scores = jnp.concatenate(
        [
            lax.dot_general(
                query_ref[0],
                out_ref[i, :tokens, :],
                (((1,), (1,)), ((), ())),
                preferred_element_type=jnp.float32,
            )
            for i in range(PAGES_STEP)
        ],
        axis=1,
    ) * HD ** (-0.5)
    row = lax.broadcasted_iota(jnp.int32, scores.shape, 0)
    start = base_ref[0] + first * tokens
    position = start + lax.broadcasted_iota(jnp.int32, scores.shape, 1)
    decode_step = lax.rem(row // GROUP, STEPS)
    limit = jnp.full(scores.shape, length_ref[seq * STEPS], jnp.int32)
    for e in range(1, STEPS):
        limit = jnp.where(decode_step == e, length_ref[seq * STEPS + e], limit)
    usable = position < limit
    old_peak = peak_ref[...]
    best = jnp.max(jnp.where(usable, scores, masked_score), axis=1, keepdims=True)
    peak = jnp.maximum(old_peak, best)
    factor = jnp.exp(old_peak - peak)
    weights = jnp.where(usable, jnp.exp(scores - peak[:, :1]), 0.0)
    denominator = denominator_ref[...] * factor + jnp.sum(weights, axis=1, keepdims=True)
    peak_ref[...] = peak
    denominator_ref[...] = denominator
    high = weights.astype(jnp.bfloat16)
    low = (weights - high.astype(jnp.float32)).astype(jnp.bfloat16)
    rows = STEPS * GROUP
    for v in range(KVH):
        part = slice(v * rows, (v + 1) * rows)
        both = jnp.concatenate([high[part], low[part]], axis=0)
        product = sum(
            jnp.dot(
                both[:, i * tokens : (i + 1) * tokens],
                out_ref[i, tokens:, v * HD : (v + 1) * HD],
                preferred_element_type=jnp.float32,
            )
            for i in range(PAGES_STEP)
        )
        numerator_ref[0, part, :] = (
            numerator_ref[0, part, :] * factor[part] + product[:rows] + product[rows:]
        )

    @pl.when(first == page_local - PAGES_STEP)
    def _():
        lane = lax.broadcasted_iota(jnp.int32, stat_ref.shape, 1)
        spot = lane // (LANES // 4)
        stats = jnp.where(spot == 2 * seq, peak, stat_ref[...])
        stat_ref[...] = jnp.where(spot == 2 * seq + 1, denominator, stats)


def attend(flags, places, kept, lengths, base, pages, resident, queries, seqs):
    total, rows, width = resident.shape
    page_local = total // seqs
    heads = KVH * STEPS * GROUP
    steps_seq = page_local // PAGES_STEP

    def page_spec(which, i):
        return pl.BlockSpec(
            (1, rows, width), lambda s, *scalars: (scalars[which][s * PAGES_STEP + i], 0, 0)
        )

    grid_spec = pltpu.PrefetchScalarGridSpec(
        num_scalar_prefetch=5,
        grid=(total // PAGES_STEP,),
        in_specs=[page_spec(1, i) for i in range(PAGES_STEP)]
        + [page_spec(2, i) for i in range(PAGES_STEP)]
        + [pl.BlockSpec((1, heads, KVH * HD), lambda s, *scalars: (s // steps_seq, 0, 0))],
        out_specs=[
            pl.BlockSpec((PAGES_STEP, rows, width), lambda s, *scalars: (s, 0, 0)),
            pl.BlockSpec((1, heads, HD), lambda s, *scalars: (s // steps_seq, 0, 0)),
            pl.BlockSpec((heads, LANES), lambda s, *scalars: (0, 0)),
        ],
        scratch_shapes=[pltpu.VMEM((heads, LANES), jnp.float32)] * 2,
    )
    return pl.pallas_call(
        functools.partial(attend_kernel, page_local),
        grid_spec=grid_spec,
        out_shape=[
            jax.ShapeDtypeStruct(resident.shape, resident.dtype),
            jax.ShapeDtypeStruct((seqs, heads, HD), jnp.float32),
            jax.ShapeDtypeStruct((heads, LANES), jnp.float32),
        ],
        compiler_params=pltpu.CompilerParams(vmem_limit_bytes=58 * MIB),
        name="attend",
    )(
        flags, places, kept, lengths, base,
        *[pages] * PAGES_STEP, *[resident] * PAGES_STEP, queries,
    )


def combine_kernel(tps, numerator_ref, stat_ref, out_ref, held, held_stat, send_sem, recv_sem, local_sem):
    tp = lax.axis_index("tp")
    seqs, rows = out_ref.shape[:2]
    barrier = pltpu.get_barrier_semaphore()
    for s in range(1, tps):
        pl.semaphore_signal(
            barrier, inc=1, device_id={"tp": lax.rem(tp + s, tps)}, device_id_type=MESH_ID
        )
    pl.semaphore_wait(barrier, tps - 1)
    copies = []
    for s in range(1, tps):
        peer = lax.rem(tp + s, tps)
        part = pl.ds(pl.multiple_of(peer * rows, 8), rows)
        for kind, (src, dst) in enumerate(
            ((numerator_ref.at[:, part, :], held), (stat_ref.at[part, :], held_stat))
        ):
            copies.append(
                pltpu.make_async_remote_copy(
                    src_ref=src,
                    dst_ref=dst.at[s],
                    send_sem=send_sem.at[kind, s - 1],
                    recv_sem=recv_sem.at[kind, s - 1],
                    device_id={"tp": peer},
                    device_id_type=MESH_ID,
                )
            )
    for copy in copies:
        copy.start()
    mine = pl.ds(pl.multiple_of(tp * rows, 8), rows)
    step = LANES // 4
    copies.append(
        pltpu.make_async_copy(numerator_ref.at[:, mine, :], held.at[0], local_sem.at[0])
    )
    copies.append(pltpu.make_async_copy(stat_ref.at[mine, :], held_stat.at[0], local_sem.at[1]))
    for copy in copies[-2:]:
        copy.start()
    for copy in copies:
        copy.wait()
    for seq in range(seqs):
        stats = [held_stat[s] for s in range(tps)]
        tops = [held[s, seq] for s in range(tps)]
        peaks = [part[:, 2 * seq * step : 2 * seq * step + 1] for part in stats]
        lows = [part[:, (2 * seq + 1) * step : (2 * seq + 1) * step + 1] for part in stats]
        peak = functools.reduce(jnp.maximum, peaks)
        factors = [jnp.exp(part - peak) for part in peaks]
        numerator = sum(top * factor for top, factor in zip(tops, factors))
        denominator = sum(low * factor for low, factor in zip(lows, factors))
        out_ref[seq] = (numerator / denominator).astype(out_ref.dtype)


def combine(numerator, stats, tps, collective_id):
    seqs, heads, size = numerator.shape
    rows = heads // tps
    return pl.pallas_call(
        functools.partial(combine_kernel, tps),
        out_shape=jax.ShapeDtypeStruct((seqs, rows, size), jnp.bfloat16),
        in_specs=[pl.BlockSpec(memory_space=pl.ANY)] * 2,
        out_specs=pl.BlockSpec(memory_space=pltpu.VMEM),
        scratch_shapes=[
            pltpu.VMEM((tps, seqs, rows, size), jnp.float32),
            pltpu.VMEM((tps, rows, LANES), jnp.float32),
            pltpu.SemaphoreType.DMA((2, tps - 1)),
            pltpu.SemaphoreType.DMA((2, tps - 1)),
            pltpu.SemaphoreType.DMA((2,)),
        ],
        compiler_params=pltpu.CompilerParams(collective_id=collective_id, has_side_effects=True),
        name="combine",
    )(numerator, stats)


def on_device(prompt_blocks, block_dest, block_slot, resident_cache, queries, context_length):
    insts = lax.axis_size("inst")
    tps = lax.axis_size("tp")
    me = lax.axis_index("inst")
    tp = lax.axis_index("tp")
    blocks, kinds, tokens, width = prompt_blocks.shape
    seqs, page_local = resident_cache.shape[:2]
    pages_seq = page_local * tps
    share = seqs * page_local
    prompt = prompt_blocks.reshape(blocks, kinds * tokens, width)
    plan = jnp.concatenate([block_dest, block_slot])
    plan = jnp.pad(plan[None, :], ((0, 7), (0, -plan.shape[0] % LANES)))
    groups = lax.axis_size("groups")
    plans, first = opening(plan, prompt, groups, insts, len(LEVELS) + 1)
    pairs = plans[:, 0, : 2 * blocks].reshape(groups, insts, 2, blocks).transpose(0, 2, 1, 3)
    pairs = pairs.reshape(groups, 2, insts * blocks)
    load = pairs[:, 0] // CORES * tps + pairs[:, 1] % pages_seq // page_local
    pools = jnp.arange(insts // CORES * tps, dtype=jnp.int32)
    counts = jnp.sum(load[:, :, None] == pools, axis=1, dtype=jnp.int32)
    counts = counts.reshape(groups, insts // CORES, tps)
    spill = SPILL if insts // CORES == 2 else 0
    levels = sorted(
        {(-(-share * size // LEVELS[-1][0]), extra if spill else 0) for size, extra in LEVELS}
    )
    sizes = jnp.array([size for size, _ in levels], jnp.int32)
    extras = jnp.array([extra for _, extra in levels], jnp.int32)
    full = CORES * sizes[:, None, None, None]
    over = jnp.maximum(counts[None] - full, 0)
    room = jnp.maximum(full - counts[None, :, ::-1], 0)
    short = over > jnp.minimum(CORES * extras[:, None, None, None], room)
    short = jnp.max(short.astype(jnp.int32), axis=(1, 2, 3))
    variant = jnp.sum(short)
    cap = sizes[0] + jnp.sum(short[:-1] * (sizes[1:] - sizes[:-1]))
    every = lax.dynamic_index_in_dim(pairs, lax.axis_index("groups"), 0, keepdims=False)
    dest, slot = every[0], every[1]
    total = insts * blocks
    holder = (slot % pages_seq) // page_local
    pool = (dest // CORES) * tps + holder
    order = jnp.arange(total, dtype=jnp.int32)
    rank = jnp.sum(
        jnp.logical_and(pool[:, None] == pool[None, :], order[None, :] < order[:, None]),
        axis=1,
        dtype=jnp.int32,
    )
    entry = jnp.arange(tps * share, dtype=jnp.int32)
    entry_pool = (me // CORES) * tps + entry // share
    entry_rank = (entry % share) * CORES + me % CORES
    hits = jnp.logical_and(pool[None, :] == entry_pool[:, None], rank[None, :] == entry_rank[:, None])
    limit = CORES * cap
    if spill:
        other_pool = (1 - me // CORES) * tps + entry // share
        spilled = rank[None, :] == 2 * limit - 1 - entry_rank[:, None]
        spilled = jnp.logical_and(spilled, (rank >= limit)[None, :])
        spilled = jnp.logical_and(spilled, pool[None, :] == other_pool[:, None])
        hits = jnp.logical_or(hits, spilled)
    index = jnp.sum(jnp.where(hits, order[None, :], 0), axis=1, dtype=jnp.int32)
    local = jnp.arange(share, dtype=jnp.int32)
    wanted = (local // page_local) * pages_seq + tp * page_local + local % page_local
    found = jnp.logical_and(dest[None, :] == me, slot[None, :] == wanted[:, None])
    spot = (rank % CORES) * share + rank // CORES
    if spill:
        slot_at = 2 * limit - 1 - rank
        spot_home = CORES * share + (slot_at % CORES) * spill + slot_at // CORES - cap + spill
        spot = jnp.where(rank >= limit, spot_home, spot)
    places = jnp.sum(jnp.where(found, spot[None, :], 0), axis=1, dtype=jnp.int32)
    flags = jnp.any(found, axis=1).astype(jnp.int32)

    pages = lax.switch(
        variant,
        [
            functools.partial(migrate, insts, tps, share, sent, extra, i)
            for i, (sent, extra) in enumerate(levels)
        ],
        index,
        prompt,
        first,
    )
    place_rows, kept_rows = [], []
    place_now = kept_now = jnp.zeros((PAGES_STEP,), jnp.int32)
    for row in range(share // PAGES_STEP):
        part = slice(row * PAGES_STEP, (row + 1) * PAGES_STEP)
        fresh = flags[part] > 0
        place_now = jnp.where(fresh, places[part], place_now)
        kept_now = jnp.where(fresh, kept_now, local[part])
        place_rows.append(place_now)
        kept_rows.append(kept_now)
    places, kept = jnp.concatenate(place_rows), jnp.concatenate(kept_rows)

    by_head = queries.reshape(seqs, STEPS, KVH, GROUP, HD).transpose(0, 2, 1, 3, 4)
    by_head = by_head.reshape(seqs, KVH, STEPS * GROUP, 1, HD)
    diagonal = jnp.eye(KVH, dtype=jnp.bool_)[None, :, None, :, None]
    wide = jnp.where(diagonal, by_head, jnp.zeros((), queries.dtype))
    wide = wide.reshape(seqs, KVH * STEPS * GROUP, KVH * HD)
    base = (tp * pages_seq // tps * tokens).astype(jnp.int32).reshape(1)
    resident = resident_cache.reshape(share, kinds * tokens, width * tps)
    installed, numerator, stats = attend(
        flags, places, kept, context_length, base, pages, resident, wide, seqs
    )
    merged = combine(numerator, stats, tps, len(LEVELS))
    attended = merged.reshape(seqs, KVH // tps, STEPS, GROUP, HD).transpose(0, 2, 1, 3, 4)
    attended = attended.reshape(seqs * STEPS, H * HD // tps)
    return attended, installed.reshape(resident_cache.shape)


def solution(mesh):
    in_specs = (
        P(("groups", "inst"), None, None, "tp"),
        P(("groups", "inst")),
        P(("groups", "inst")),
        P(("groups", "inst"), "tp", None, None, None),
        P(("groups", "inst"), None),
        P(("groups", "inst")),
    )
    out_specs = (P(("groups", "inst"), "tp"), P(("groups", "inst"), "tp", None, None, None))
    return jax.shard_map(
        on_device, mesh=mesh, in_specs=in_specs, out_specs=out_specs, check_vma=False
    )
```
